128 devices in a mesh: sect: 2 (over core), dev: 64 (over x, y, z).
Axes of the slice: x: 4, y: 4, z: 4, core: 2. Of those that a mesh axis runs over, the one named last changes fastest.
Arguments:
- atmosphere_state: bfloat16 [4, 72, 131072], P(None, None, ('sect', 'dev')), may hold values from -5 to 5
- metric: float32 [2, 131072], P(None, ('sect', 'dev')), may hold values from 0.05 to 0.5
- column_group_target: int32 [131072, 1], replicated, may hold values from 0 to 127; in each aligned block of 1024 rows (0 to 1023, 1024 to 2047, ...) at most 16 rows name the same one
- physics_input_layer: bfloat16 [288, 1024], replicated, may hold values from -0.375 to 0.375
- physics_tendency_layer: bfloat16 [1024, 288], replicated, may hold values from -0.1875 to 0.1875
- physics_flux_layer: bfloat16 [1024, 4], replicated, may hold values from -0.1875 to 0.1875
- block_to_tile: int32 [1024], replicated, may hold values from 0 to 1023, as said below
- remap_weight_matrix: float32 [128, 128], replicated, may hold values from -0.5 to 0.5
- ocean_land_mask: int32 [1024, 128], P(('sect', 'dev')), may hold values 0 or 1
- ocean_sea_anomaly: float32 [1024, 128], P(('sect', 'dev')), may hold values from -5 to 5
- flux_sea_response: float32 [4], replicated, may hold values from -3 to 3
Outputs:
- stepped_state: bfloat16 [4, 72, 131072], P(None, None, ('sect', 'dev'))
- group_layout_tendency: bfloat16 [262144, 288], P(('sect', 'dev'))
- updated_sea_temp: float32 [1024, 128], P(('sect', 'dev'))
- atmosphere_sea_temp: float32 [131072], P(('sect', 'dev'))
The draws below stay inside these ranges and needn't reach their ends.
Inputs may be any that keep to these rules, and one draw needn't show every extreme that they name: `column_group_target`: among the columns of one device no group is named more than 16 times; in some devices one group is named exactly 16 times. `block_to_tile`: A permutation: block j of device a (block a 8 + j) feeds tile j of device (a + s_j) mod the number of devices, with shifts s_j common to all devices; at most 2 of the shifts are equal, and exactly 2 are equal in every draw.
All inputs are finite; a program needn't handle non-finite values. No bound on the sum of `ocean_land_mask` on one device may be relied on, other than what follows from the above.
Results may differ from the reference program's by a relative error of at most 0.0068.
Values may be sent and summed in bfloat16 or wider, within the bound.
A program may use at most 128 MiB of HBM per device.

```python
import math
import jax
import jax.numpy as jnp
import numpy as np
from jax import lax

NF = 4
LEV = 72
HID = 1024
NFLUX = 4
BLOCK_CELLS = 128
COLS_DEV = 1024
COLUMN_COUNT = 131072
BLK_DEV = 8
BLOCK_COUNT = 1024
CAP = 16
SLOTS = 262144
N_SECT = 2
N_DEV = 64


def draw_block_to_tile(key, part):
    key = jax.random.fold_in(key, 11)
    key_shift, key_order = jax.random.split(key)
    devices = BLOCK_COUNT // BLK_DEV
    groups = jnp.concatenate([jnp.array([0, 0, 1, 1], jnp.int32), jnp.arange(2, BLK_DEV - 2, dtype=jnp.int32)])
    shifts = jax.random.permutation(key_shift, devices)[groups]
    shifts = shifts[jax.random.permutation(key_order, BLK_DEV)]
    owners = (jnp.arange(devices, dtype=jnp.int32)[:, None] + shifts[None, :].astype(jnp.int32)) % devices
    tiles = owners * BLK_DEV + jnp.arange(BLK_DEV, dtype=jnp.int32)[None, :]
    return tiles.reshape(-1).astype(jnp.int32)


def set_ends(values, key, least, largest):
    extent = values.shape
    place = [jax.random.randint(jax.random.fold_in(key, axis), (), 0, extent[axis]) for axis in range(len(extent))]
    values = values.at[tuple(place)].set(least)
    longest = extent.index(max(extent))
    place[longest] = (place[longest] + 1) % extent[longest]
    return values.at[tuple(place)].set(largest)


def level_of(own_key, shape, cuts, smallest, top_value):
    level = 1.0
    for dim, parts in cuts:
        heights = jax.random.uniform(jax.random.fold_in(jax.random.fold_in(own_key, 6), dim), (parts,), jnp.float32, smallest / len(cuts), top_value / len(cuts))
        level = level * jnp.repeat(jnp.exp(heights), shape[dim] // parts).reshape((-1,) + (1,) * (len(shape) - 1 - dim))
    return level


def shared_out(own_key, own, number, rows, amount, top, bound, lean):
    ranking = jax.random.permutation(own_key, amount)
    packed, usual = load_shares(amount, rows * top, bound, lean, True), load_shares(amount, rows * top, bound, lean, False)
    places = jnp.arange(amount)

    def named(tallies, rotation):
        used = int((tallies > 0).sum())
        fixed = max(1, used // 4)
        passed = fixed + (places - fixed + rotation * (used - fixed)) % max(1, amount - fixed)
        return jnp.zeros((amount,), jnp.int32).at[ranking[jnp.where(places < fixed, places, passed)]].set(jnp.asarray(tallies, jnp.int32))

    tallies = jnp.where(number % 4 == 0, named(packed, number // 4), named(usual, number - number // 4 - 1))
    mixed = jax.random.permutation(jax.random.fold_in(own, 3), amount)
    donor, sink = mixed[0:amount // 2 * 2:2], mixed[1:amount // 2 * 2:2]
    room = jnp.minimum(tallies[donor] - 1, bound - tallies[sink]) // 2
    room = jnp.where((donor == ranking[0]) | (sink == ranking[0]) | (tallies[sink] == 0), 0, jnp.maximum(room, 0))
    passed = jax.random.randint(jax.random.fold_in(own, 4), (amount // 2,), 0, 1 << 20) % (room + 1)
    tallies = tallies.at[donor].add(-passed).at[sink].add(passed)
    members = jnp.searchsorted(jnp.cumsum(tallies), jnp.arange(rows * top), side="right").astype(jnp.int32)
    grid = members.reshape(top, rows).T
    grid = grid[jax.random.permutation(jax.random.fold_in(own, 1), rows)]
    rotation = jax.random.randint(jax.random.fold_in(own, 2), (rows, 1), 0, top)
    return jnp.take_along_axis(grid, (jnp.arange(top)[None, :] + rotation) % top, axis=1)


def load_shares(count, total, limit, skew, full):
    portions = [(1 << 20) // math.isqrt(rank ** skew) + 1 for rank in range(1, count + 1)]
    largest = limit if full else min(limit, max(-(-total // count), total * portions[0] // sum(portions)))
    least = 1 if total - largest >= count - 1 else 0
    holding, rest = [largest] + [least] * (count - 1), total - largest - least * (count - 1)
    while rest > 0:
        movable = [i for i in range(1, count) if holding[i] < largest] or [i for i in range(1, count) if holding[i] < limit]
        whole, remaining = sum([portions[i] for i in movable]), rest
        for i in movable:
            addition = min(limit - holding[i], max(1, remaining * portions[i] // whole), rest)
            holding[i] = holding[i] + addition
            rest = rest - addition
    return np.array(holding)


def noise(stream_key, extent, width, reach, cuts=(), kind=jnp.bfloat16):
    result = width * jax.random.normal(stream_key, extent, jnp.float32)
    if cuts:
        result = result * level_of(stream_key, extent, cuts, -0.22, 0.18)
    return jnp.clip(result, -reach, reach).astype(kind)


def setup_inputs(seed: int = 0) -> dict:
    seeds = jax.random.split(jax.random.key(seed), 12)
    atmosphere_state = noise(seeds[0], (NF, LEV, COLUMN_COUNT), 1.0, 5.0, ((2, 128),))
    metric = jnp.clip(jnp.exp(math.log(0.5) - 2.3025851 * jax.random.uniform(seeds[1], (2, COLUMN_COUNT), jnp.float32) ** level_of(seeds[1], (2, COLUMN_COUNT), ((1, 128),), -0.2, 0.2)), 0.05, 0.5)
    column_group_target_keys = jax.random.split(jax.random.fold_in(seeds[2], 1), COLUMN_COUNT // COLS_DEV)
    column_group_target_turns = jax.random.permutation(jax.random.fold_in(seeds[2], 3), COLUMN_COUNT // COLS_DEV)
    column_group_target = jax.vmap(lambda own, number: shared_out(jax.random.fold_in(seeds[2], 2), own, number, COLS_DEV, N_SECT * N_DEV, 1, CAP, 2))(column_group_target_keys, column_group_target_turns).reshape((COLUMN_COUNT, 1))
    physics_input_layer = noise(seeds[3], (NF * LEV, HID), (NF * LEV) ** -0.5, 0.375)
    physics_tendency_layer = noise(seeds[4], (HID, NF * LEV), HID ** -0.5, 0.1875)
    physics_flux_layer = noise(seeds[5], (HID, NFLUX), HID ** -0.5, 0.1875)
    block_to_tile = draw_block_to_tile(jax.random.fold_in(seeds[11], 71), 0)
    remap_weight_matrix = noise(seeds[7], (BLOCK_CELLS, BLOCK_CELLS), BLOCK_CELLS ** -0.5, 0.5, (), jnp.float32)
    ocean_land_mask = set_ends((jax.random.randint(seeds[8], (BLOCK_COUNT, BLOCK_CELLS), 0, 10) < 7).astype(jnp.int32), jax.random.fold_in(seeds[8], 1), 0, 1)
    ocean_sea_anomaly = noise(seeds[9], (BLOCK_COUNT, BLOCK_CELLS), 1.0, 5.0, ((0, 128),), jnp.float32)
    flux_sea_response = noise(seeds[10], (NFLUX,), 1.0, 3.0, (), jnp.float32)
    return dict(atmosphere_state=atmosphere_state, metric=metric, column_group_target=column_group_target, physics_input_layer=physics_input_layer, physics_tendency_layer=physics_tendency_layer, physics_flux_layer=physics_flux_layer, block_to_tile=block_to_tile, remap_weight_matrix=remap_weight_matrix, ocean_land_mask=ocean_land_mask, ocean_sea_anomaly=ocean_sea_anomaly, flux_sea_response=flux_sea_response)


def gll_tables():
    gll_nodes = np.array([-1.0, -1.0 / np.sqrt(5.0), 1.0 / np.sqrt(5.0), 1.0])
    offdiag = gll_nodes[:, None] - gll_nodes[None, :] + np.eye(4)
    bary = np.prod(offdiag, axis=1)
    derivative = bary[:, None] / (bary[None, :] * offdiag)
    diag_sum = np.sum(1.0 / offdiag - np.eye(4), axis=1)
    derivative = derivative * (1.0 - np.eye(4)) + np.eye(4) * diag_sum[:, None]
    first_dir = np.kron(np.eye(8), np.kron(np.eye(4), derivative)).T
    second_dir = np.kron(np.eye(8), np.kron(derivative, np.eye(4))).T
    return (jnp.asarray(first_dir, jnp.float32).astype(jnp.bfloat16), jnp.asarray(second_dir, jnp.float32).astype(jnp.bfloat16))

def dynamics(atmosphere_state, metric):
    first_dir, second_dir = gll_tables()
    array_shape = atmosphere_state.shape
    flat = atmosphere_state.reshape(-1, 128)
    grad_first = jnp.dot(flat, first_dir, preferred_element_type=jnp.float32).reshape(array_shape)
    grad_second = jnp.dot(flat, second_dir, preferred_element_type=jnp.float32).reshape(array_shape)
    wind_first = (atmosphere_state[0].astype(jnp.float32) * metric[0][None, :])[None]
    wind_second = (atmosphere_state[1].astype(jnp.float32) * metric[1][None, :])[None]
    advected = atmosphere_state.astype(jnp.float32) - wind_first * grad_first - wind_second * grad_second
    return advected.astype(jnp.bfloat16)

def physics(columns, physics_input_layer, physics_tendency_layer, physics_flux_layer):
    hidden = jax.nn.silu(jnp.dot(columns, physics_input_layer, preferred_element_type=jnp.float32)).astype(jnp.bfloat16)
    tendency = jnp.dot(hidden, physics_tendency_layer, preferred_element_type=jnp.float32)
    updated = (columns.astype(jnp.float32) + tendency).astype(jnp.bfloat16)
    fluxes = jnp.dot(hidden, physics_flux_layer, preferred_element_type=jnp.float32).astype(jnp.bfloat16)
    return (updated, tendency.astype(jnp.bfloat16), fluxes)

def reference(atmosphere_state, metric, column_group_target, physics_input_layer, physics_tendency_layer, physics_flux_layer, block_to_tile, remap_weight_matrix, ocean_land_mask, ocean_sea_anomaly, flux_sea_response):
    devices = N_SECT * N_DEV
    col_width = NF * LEV
    advected = dynamics(atmosphere_state, metric)
    columns = advected.reshape(col_width, COLUMN_COUNT).T.reshape(devices, COLS_DEV, col_width)
    updated, tendency, fluxes = lax.map(lambda group: physics(group, physics_input_layer, physics_tendency_layer, physics_flux_layer), columns)
    updated = updated.reshape(COLUMN_COUNT, col_width)
    tendency = tendency.reshape(COLUMN_COUNT, col_width)
    fluxes = fluxes.reshape(COLUMN_COUNT, NFLUX)
    stepped_state = updated.T.reshape(NF, LEV, COLUMN_COUNT)
    targets = column_group_target[:, 0].reshape(devices, COLS_DEV)

    def positions(row_targets):
        onehot = (row_targets[:, None] == jnp.arange(devices, dtype=jnp.int32)[None, :]).astype(jnp.int32)
        earlier = jnp.cumsum(onehot, axis=0) - onehot
        return lax.optimization_barrier(jnp.sum(earlier * onehot, axis=1)).astype(jnp.int32)
    position = lax.map(positions, targets)
    sources = jnp.arange(devices, dtype=jnp.int32)[:, None]
    rows_index = (targets * (2 * COLS_DEV) + sources * CAP + position).reshape(-1)
    group_layout_tendency = jnp.zeros((SLOTS, col_width), jnp.bfloat16).at[rows_index].set(tendency)
    block_fluxes = fluxes.T.reshape(NFLUX, BLOCK_COUNT, BLOCK_CELLS).astype(jnp.float32)
    inverse = jnp.zeros((BLOCK_COUNT,), jnp.int32).at[block_to_tile].set(jnp.arange(BLOCK_COUNT, dtype=jnp.int32))
    source_flux = block_fluxes[:, inverse]
    mask_as_float = ocean_land_mask.astype(jnp.float32)
    cell_surface_flux = mask_as_float[None] * jnp.einsum('im,ktm->kti', remap_weight_matrix, source_flux, precision=lax.Precision.HIGHEST)
    updated_sea_temp = ocean_sea_anomaly + jnp.einsum('l,leu->eu', flux_sea_response, cell_surface_flux, precision=lax.Precision.HIGHEST)
    ocean_cell_sea_temp = mask_as_float * updated_sea_temp
    atmosphere_sea_temp = jnp.einsum('xn,kx->kn', remap_weight_matrix, ocean_cell_sea_temp[block_to_tile], precision=lax.Precision.HIGHEST).reshape(COLUMN_COUNT)
    return (stepped_state, group_layout_tendency, updated_sea_temp, atmosphere_sea_temp)
```

```python
import functools
import itertools
import random

import jax
import jax.numpy as jnp
import numpy as np
from jax import lax
from jax.experimental import pallas as pl
from jax.experimental.pallas import tpu as pltpu
from jax.sharding import PartitionSpec as P

MESH = pl.DeviceIdType.MESH
BF16 = jnp.bfloat16
F32 = jnp.float32
I32 = jnp.int32

DEVICES = 128
CAP = 16
COLS = 1024
WIDTH = 288
HID = 1024
ROWS = 40
STEP = 256
PART = 512
NT = (((1,), (1,)), ((), ()))


def gll_tables():
    gll_nodes = np.array([-1.0, -1.0 / np.sqrt(5.0), 1.0 / np.sqrt(5.0), 1.0])
    offdiag = gll_nodes[:, None] - gll_nodes[None, :] + np.eye(4)
    bary = np.prod(offdiag, axis=1)
    derivative = bary[:, None] / (bary[None, :] * offdiag)
    diag_sum = np.sum(1.0 / offdiag - np.eye(4), axis=1)
    derivative = derivative * (1.0 - np.eye(4)) + np.eye(4) * diag_sum[:, None]
    first_dir = np.kron(np.eye(8), np.kron(np.eye(4), derivative)).T
    second_dir = np.kron(np.eye(8), np.kron(derivative, np.eye(4))).T
    both = np.concatenate([first_dir, second_dir], axis=1)
    return jnp.asarray(both, F32).astype(BF16)


def message_order():
    hops = lambda k: min(k, 4 - k)
    offsets = list(itertools.product(range(2), range(4), range(4), range(4)))
    random.Random(1).shuffle(offsets)
    offsets.sort(key=lambda o: (-sum(hops(k) for k in o[1:]), o == (0, 0, 0, 0)))
    here = offsets.index((0, 0, 0, 0))
    offsets.append(offsets.pop(here))
    return offsets


ORDER = message_order()


def device(index):
    return (lax.div(index, 64), lax.rem(index, 64))


def dot(a, b):
    return jnp.dot(a, b, preferred_element_type=F32)


def dot_nt(a, b, precision=None):
    return lax.dot_general(a, b, NT, precision=precision, preferred_element_type=F32)


def iota(shape, dim):
    return lax.broadcasted_iota(I32, shape, dim)


def one_hot(condition):
    return jnp.where(condition, 1.0, 0.0).astype(BF16)


def kernel(
    state_hbm,
    target_hbm,
    w1_hbm,
    w2t_hbm,
    metric_ref,
    w3t_ref,
    tile_ref,
    remap_ref,
    mask_ref,
    anomaly_ref,
    response_ref,
    deriv_ref,
    order_ref,
    stepped_hbm,
    layout_hbm,
    updated_ref,
    atmos_ref,
    x_v,
    target_v,
    w1_v,
    w1t_v,
    w23_v,
    adv_v,
    hid_v,
    tend_v,
    step_v,
    lay_v,
    q_v,
    send_v,
    recv_v,
    near_send,
    near_recv,
    far_send,
    far_recv,
    in_sem,
    out_sem,
    lay_sem,
    send_sem,
    recv_sem,
    near_sem,
    far_sem,
):
    core, chip = lax.axis_index("sect"), lax.axis_index("dev")
    me = core * 64 + chip
    high, low = lax.div(me, 8), lax.rem(me, 8)

    loads = [
        pltpu.make_async_copy(target_hbm.at[me], target_v, in_sem.at[0]),
        pltpu.make_async_copy(w1_hbm, w1_v, in_sem.at[1]),
        pltpu.make_async_copy(state_hbm, x_v, in_sem.at[2]),
        pltpu.make_async_copy(w2t_hbm, w23_v.at[pl.ds(0, WIDTH)], in_sem.at[3]),
    ]
    for load in loads:
        load.start()

    barrier = pltpu.get_barrier_semaphore()

    @pl.loop(1, DEVICES, unroll=4)
    def _(i):
        pl.semaphore_signal(
            barrier, inc=1, device_id=device(lax.rem(me + 64 + i + lax.div(i, 64), DEVICES)), device_id_type=MESH
        )

    lane, sub = iota((8, 128), 1), iota((8, 128), 0)
    tile8 = tile_ref[0:1, :]
    shift_row = jnp.where(iota((1, 128), 1) < 8, tile8 >> 3, -1)
    shift_col = jnp.sum(jnp.where(lane == sub, shift_row, 0), axis=1, keepdims=True)
    same = jnp.where((shift_row == shift_col) & (lane < 8), 1, 0)
    twin_row = jnp.sum(jnp.where(sub < lane, same, 0), axis=0, keepdims=True)
    twin_col = jnp.sum(jnp.where(lane < sub, same, 0), axis=1, keepdims=True)

    order = order_ref[...]
    x, y, z = lax.div(chip, 16), lax.rem(lax.div(chip, 4), 4), lax.rem(chip, 4)
    to_device = (
        ((order[:, 0:1] + core) & 1) * 64
        + ((order[:, 1:2] + x) & 3) * 16
        + ((order[:, 2:3] + y) & 3) * 4
        + ((order[:, 3:4] + z) & 3)
    )

    loads[0].wait()
    targets = jnp.concatenate([target_v[k : k + 1, :] for k in range(8)], axis=1)
    before = one_hot(iota((STEP, STEP), 0) < iota((STEP, STEP), 1))
    message = iota((DEVICES, STEP), 0)
    taken = jnp.zeros((DEVICES, 1), F32)
    slots = []
    for c in range(COLS // STEP):
        hit = to_device == targets[:, c * STEP : (c + 1) * STEP]
        hits = jnp.where(hit, 1.0, 0.0)
        earlier = dot(hits.astype(BF16), before) + taken
        taken = taken + jnp.sum(hits, axis=1, keepdims=True)
        slot = jnp.where(hit, earlier.astype(I32) + CAP * message, 0)
        slots.append(jnp.sum(slot, axis=0, keepdims=True))
    slots = jnp.concatenate(slots, axis=1)

    ocean = mask_ref[...].astype(F32)
    ahead = jnp.concatenate([ocean, ocean * anomaly_ref[...]], axis=0).astype(BF16)
    near_send[...] = ahead
    near_recv[low] = ahead

    loads[1].wait()
    unit = one_hot(iota((256, 256), 0) == iota((256, 256), 1))
    for b in range(HID // 256):
        rows = slice(b * 256, (b + 1) * 256)
        w1t_v[rows, :] = dot_nt(unit, w1_v[:, rows]).astype(BF16)
    loads[3].wait()
    w23_v[WIDTH : WIDTH + 16, :] = jnp.concatenate([w3t_ref[...].astype(F32), jnp.zeros((12, HID), F32)], axis=0).astype(BF16)

    loads[2].wait()
    deriv = deriv_ref[...]
    stores = []
    for c in range(COLS // STEP):
        for b in range(STEP // 128):
            at = slice(c * STEP + b * 128, c * STEP + (b + 1) * 128)
            field = x_v[:, at]
            grads = dot(field, deriv)
            wide = field.astype(F32)
            wind_first = wide[0:72] * metric_ref[0:1, at]
            wind_second = wide[72:144] * metric_ref[1:2, at]
            moved = (
                wide
                - jnp.concatenate([wind_first] * 4, axis=0) * grads[:, 0:128]
                - jnp.concatenate([wind_second] * 4, axis=0) * grads[:, 128:256]
            )
            adv_v[:, at] = moved.astype(BF16)
        at = slice(c * STEP, (c + 1) * STEP)
        column = adv_v[:, at]
        for b in range(HID // 256):
            rows = slice(b * 256, (b + 1) * 256)
            pre = dot(w1t_v[rows, :], column)
            hid_v[rows, at] = (0.5 * pre * (1.0 + jnp.tanh(0.5 * pre))).astype(BF16)
        result = dot(w23_v[...], hid_v[:, at])
        tendency = result[0:WIDTH]
        step_v[:, at] = (column.astype(F32) + tendency).astype(BF16)
        tendency = tendency.astype(BF16)
        tend_v[0:WIDTH, at] = tendency
        for g in range(1, 4):
            tend_v[256 + 32 * g : 288 + 32 * g, at] = tendency[256:288]
        flux = result[WIDTH : WIDTH + 8].astype(BF16).astype(F32)
        mixed = sum(response_ref[k] * flux[k : k + 1] for k in range(4))
        for b in range(STEP // 128):
            j = c * (STEP // 128) + b
            q_v[j : j + 1, :] = mixed[:, b * 128 : (b + 1) * 128]
        store = pltpu.make_async_copy(step_v.at[:, at], stepped_hbm.at[:, at], out_sem.at[c])
        store.start()
        stores.append(store)

    q = q_v[...]
    q_rows = jnp.concatenate([q, jnp.zeros((120, 128), F32)], axis=0).astype(BF16)
    flux_to = jnp.where(shift_row < 0, -1, (shift_row + me) & (DEVICES - 1))
    flux_rows = [dot(one_hot((to_device == flux_to) & (twin_row == u)), q_rows) for u in range(2)]

    pl.semaphore_wait(barrier, DEVICES - 1)

    @pl.loop(1, 8)
    def _(i):
        peer = high * 8 + lax.rem(low + i, 8)
        pltpu.make_async_remote_copy(
            near_send, near_recv.at[low], near_sem.at[0], near_sem.at[1], device_id=device(peer), device_id_type=MESH
        ).start()

    cores = [lax.rem(core + k, 2) for k in range(2)]
    xs = [lax.rem(x + k, 4) * 16 for k in range(4)]
    ys = [lax.rem(y + k, 4) * 4 for k in range(4)]
    zs = [lax.rem(z + k, 4) for k in range(4)]
    here = pltpu.make_async_copy(send_v.at[DEVICES - 1], recv_v.at[me], recv_sem.at[high])
    packed_row = iota((PART // CAP, 8, 128), 1)
    keep = (iota((PART, 128), 0) & 15) >> 2 == iota((PART, 128), 1) >> 5
    for k in range(DEVICES * CAP // PART):
        pick = one_hot(iota((PART, COLS), 0) + k * PART == slots)
        placed = dot_nt(pick, tend_v[...])
        first, count = k * PART // CAP, PART // CAP
        into = pl.ds(first, count)
        main = placed[:, 0:256].astype(BF16)
        send_v[into, 0:16, :] = main[:, 0:128].reshape(count, CAP, 128)
        send_v[into, 16:32, :] = main[:, 128:256].reshape(count, CAP, 128)
        tail = jnp.where(keep, placed[:, 256:384], 0.0).reshape(count, CAP, 128)
        tail = tail[:, 0:8] + tail[:, 8:16]
        tail = tail + jnp.concatenate([tail[:, 4:8], tail[:, 0:4]], axis=1)
        for u in range(2):
            row = flux_rows[u][first : first + count].reshape(count, 1, 128)
            tail = jnp.where(packed_row == 4 + u, row, tail)
        send_v[into, 32:40, :] = tail.astype(BF16)
        for i in range(first, first + count):
            if i == DEVICES - 1:
                here.start()
                continue
            a, b, e, f = ORDER[i]
            pltpu.make_async_remote_copy(
                send_v.at[i],
                recv_v.at[me],
                send_sem,
                recv_sem.at[high],
                device_id=(cores[a], xs[b] + ys[e] + zs[f]),
                device_id_type=MESH,
            ).start()
        if k == 1:
            got = near_recv.at[pl.ds(0, 7)]
            pltpu.make_async_copy(got, got, near_sem.at[1]).wait()
            source = (low + shift_col) & 7
            source = jnp.concatenate([source, source], axis=0)
            chosen = jnp.zeros((16, 128), F32)
            for l in range(8):
                chosen = chosen + jnp.where(source == l, near_recv[l].astype(F32), 0.0)
            chosen = chosen.astype(BF16)
            far_send[...] = chosen
            far_recv[high] = chosen

            @pl.loop(1, 16)
            def _(i):
                peer = lax.rem(high + i, 16) * 8 + low
                pltpu.make_async_remote_copy(
                    far_send, far_recv.at[high], far_sem.at[0], far_sem.at[1], device_id=device(peer), device_id_type=MESH
                ).start()

    got = far_recv.at[pl.ds(0, 15)]
    pltpu.make_async_copy(got, got, far_sem.at[1]).wait()
    source = ((me + shift_col) & (DEVICES - 1)) >> 3
    source = jnp.concatenate([source, source], axis=0)
    chosen = jnp.zeros((16, 128), F32)
    for h in range(16):
        chosen = chosen + jnp.where(source == h, far_recv[h].astype(F32), 0.0)
    remap = remap_ref[...]
    cell = dot_nt(q, remap, lax.Precision.HIGHEST)
    masked = chosen[8:16] + chosen[0:8] * cell
    atmos_ref[...] = jnp.dot(masked, remap, precision=lax.Precision.HIGHEST, preferred_element_type=F32)

    unit = one_hot(iota((128, 128), 0) == iota((128, 128), 1))
    slot, row = iota((128, 64), 0), iota((128, 64), 1)
    spread = one_hot((row >> 3 == slot >> 4) & ((row & 7) == (slot & 3)))
    held = (iota((128, 128), 0) & 15) >> 2 == iota((128, 128), 1) >> 5
    fold = one_hot(iota((32, 128), 0) == (iota((32, 128), 1) & 31))
    flux_row = ((me - shift_col) & (DEVICES - 1)) * 8 + 4 + twin_col
    q_v[...] = jnp.zeros((8, 128), F32)

    @pl.loop(0, 16)
    def _(n):
        group = lax.rem(high + 8 + n, 16)
        eight = pl.ds(pl.multiple_of(group * 8, 8), 8)
        got = recv_v.at[eight]
        pltpu.make_async_copy(got, got, recv_sem.at[group]).wait()
        lanes = pl.ds(pl.multiple_of(group * 128, 128), 128)
        for half in range(2):
            part = recv_v[eight, 16 * half : 16 * half + 16, :].reshape(128, 128)
            lay_v[128 * half : 128 * half + 128, lanes] = dot_nt(unit, part).astype(BF16)
        packed = recv_v[eight, 32:40, :].astype(F32).reshape(64, 128).astype(BF16)
        wide = jnp.where(held, dot(spread, packed), 0.0).astype(BF16)
        lay_v[256:288, lanes] = dot_nt(fold, wide).astype(BF16)
        q_v[...] += dot(one_hot(iota((8, 64), 1) + group * 64 == flux_row), packed)
        pltpu.make_async_copy(lay_v.at[:, lanes], layout_hbm.at[:, lanes], lay_sem).start()

    cell = dot_nt(q_v[...], remap, lax.Precision.HIGHEST)
    updated_ref[...] = anomaly_ref[...] + mask_ref[...].astype(F32) * cell

    for store in stores:
        store.wait()
    pltpu.make_async_copy(lay_v, layout_hbm, lay_sem).wait()
    sent = send_v.at[pl.ds(0, DEVICES - 1)]
    pltpu.make_async_copy(sent, sent, send_sem).wait()
    sent = near_recv.at[pl.ds(0, 7)]
    pltpu.make_async_copy(sent, sent, near_sem.at[0]).wait()
    sent = far_recv.at[pl.ds(0, 15)]
    pltpu.make_async_copy(sent, sent, far_sem.at[0]).wait()


def per_device(
    atmosphere_state,
    metric,
    column_group_target,
    physics_input_layer,
    physics_tendency_layer,
    physics_flux_layer,
    block_to_tile,
    remap_weight_matrix,
    ocean_land_mask,
    ocean_sea_anomaly,
    flux_sea_response,
):
    anywhere, vmem = pl.BlockSpec(memory_space=pl.ANY), pl.BlockSpec(memory_space=pltpu.VMEM)
    smem = pl.BlockSpec(memory_space=pltpu.SMEM)
    order = np.zeros((DEVICES, 8), np.int32)
    order[:, :4] = ORDER
    stepped, layout, updated, atmos = pl.pallas_call(
        kernel,
        out_shape=[
            jax.ShapeDtypeStruct((WIDTH, COLS), BF16),
            jax.ShapeDtypeStruct((WIDTH, DEVICES * CAP), BF16),
            jax.ShapeDtypeStruct((8, 128), F32),
            jax.ShapeDtypeStruct((8, 128), F32),
        ],
        in_specs=[anywhere] * 4 + [vmem] * 6 + [smem] + [vmem] * 2,
        out_specs=[anywhere, anywhere, vmem, vmem],
        scratch_shapes=[
            pltpu.VMEM((WIDTH, COLS), BF16),
            pltpu.VMEM((8, 128), I32),
            pltpu.VMEM((WIDTH, HID), BF16),
            pltpu.VMEM((HID, WIDTH), BF16),
            pltpu.VMEM((WIDTH + 16, HID), BF16),
            pltpu.VMEM((WIDTH, COLS), BF16),
            pltpu.VMEM((HID, COLS), BF16),
            pltpu.VMEM((384, COLS), BF16),
            pltpu.VMEM((WIDTH, COLS), BF16),
            pltpu.VMEM((WIDTH, DEVICES * CAP), BF16),
            pltpu.VMEM((8, 128), F32),
            pltpu.VMEM((DEVICES, ROWS, 128), BF16),
            pltpu.VMEM((DEVICES, ROWS, 128), BF16),
            pltpu.VMEM((16, 128), BF16),
            pltpu.VMEM((8, 16, 128), BF16),
            pltpu.VMEM((16, 128), BF16),
            pltpu.VMEM((16, 16, 128), BF16),
            pltpu.SemaphoreType.DMA((4,)),
            pltpu.SemaphoreType.DMA((COLS // STEP,)),
            pltpu.SemaphoreType.DMA,
            pltpu.SemaphoreType.DMA,
            pltpu.SemaphoreType.DMA((16,)),
            pltpu.SemaphoreType.DMA((2,)),
            pltpu.SemaphoreType.DMA((2,)),
        ],
        compiler_params=pltpu.CompilerParams(
            collective_id=0, has_side_effects=True, vmem_limit_bytes=48 * 1024 * 1024
        ),
        name="coupling_interval",
    )(
        atmosphere_state.reshape(WIDTH, COLS),
        column_group_target.reshape(DEVICES, 8, 128),
        physics_input_layer,
        physics_tendency_layer.T,
        metric,
        physics_flux_layer.T,
        block_to_tile.reshape(8, 128),
        remap_weight_matrix,
        ocean_land_mask,
        ocean_sea_anomaly,
        flux_sea_response,
        gll_tables(),
        jnp.asarray(order),
    )
    return (
        stepped.reshape(atmosphere_state.shape),
        layout.T,
        updated,
        atmos.reshape(COLS),
    )


def solution(mesh):
    placed = (
        P(None, None, ("sect", "dev")),
        P(None, ("sect", "dev")),
        P(),
        P(),
        P(),
        P(),
        P(),
        P(),
        P(("sect", "dev"), None),
        P(("sect", "dev"), None),
        P(),
    )
    return jax.shard_map(
        per_device,
        mesh=mesh,
        in_specs=placed,
        out_specs=(
            P(None, None, ("sect", "dev")),
            P(("sect", "dev"), None),
            P(("sect", "dev"), None),
            P(("sect", "dev")),
        ),
        check_vma=False,
    )
```

```python
import functools
import itertools
import random

import jax
import jax.numpy as jnp
import numpy as np
from jax import lax
from jax.experimental import pallas as pl
from jax.experimental.pallas import tpu as pltpu
from jax.sharding import PartitionSpec as P

MESH = pl.DeviceIdType.MESH
BF16 = jnp.bfloat16
F32 = jnp.float32
I32 = jnp.int32

DEVICES = 128
CAP = 16
COLS = 1024
WIDTH = 288
HID = 1024
ROWS = 40
STEP = 256
VMEM_LIMIT = 32 * 1024 * 1024
NT = (((1,), (1,)), ((), ()))


def gll_tables():
    gll_nodes = np.array([-1.0, -1.0 / np.sqrt(5.0), 1.0 / np.sqrt(5.0), 1.0])
    offdiag = gll_nodes[:, None] - gll_nodes[None, :] + np.eye(4)
    bary = np.prod(offdiag, axis=1)
    derivative = bary[:, None] / (bary[None, :] * offdiag)
    diag_sum = np.sum(1.0 / offdiag - np.eye(4), axis=1)
    derivative = derivative * (1.0 - np.eye(4)) + np.eye(4) * diag_sum[:, None]
    first_dir = np.kron(np.eye(8), np.kron(np.eye(4), derivative)).T
    second_dir = np.kron(np.eye(8), np.kron(derivative, np.eye(4))).T
    return np.concatenate([first_dir, second_dir], axis=1)


QUARTERS = [[(0, 1), (0, 3)], [(1, 1), (1, 3)], [(0, 2), (0, 0)], [(1, 2), (1, 0)]]


def message_order():
    hops = lambda k: min(k, 4 - k)
    mixed, order = random.Random(1), []
    for planes in QUARTERS:
        part = [plane + yz for plane in planes for yz in itertools.product(range(4), range(4))]
        mixed.shuffle(part)
        part.sort(key=lambda o: (o == SELF, -sum(hops(k) for k in o[1:])))
        order += part
    return order


SELF = (0, 0, 0, 0)
ORDER = message_order()
FAR_FIRST = sorted(ORDER, key=lambda o: -sum(min(k, 4 - k) for k in o[1:]))
CHUNKS = [8, 24, 32, 32, 32]


def tables():
    table = np.zeros((DEVICES, 384), np.float32)
    table[:, :256] = gll_tables()
    table[:, 256:260] = ORDER
    return table


def device(index):
    return (lax.div(index, 64), lax.rem(index, 64))


def dot(a, b):
    return jnp.dot(a, b, preferred_element_type=F32)


def dot_nt(a, b, precision=None):
    return lax.dot_general(a, b, NT, precision=precision, preferred_element_type=F32)


def iota(shape, dim):
    return lax.broadcasted_iota(I32, shape, dim)


def one_hot(condition):
    return jnp.where(condition, 1.0, 0.0).astype(BF16)


def kernel(
    target_hbm,
    table_hbm,
    w1_hbm,
    state_hbm,
    metric_hbm,
    w2t_hbm,
    w3t_hbm,
    response_hbm,
    tile_hbm,
    mask_hbm,
    anomaly_hbm,
    remap_hbm,
    stepped_out,
    layout_out,
    updated_out,
    atmos_out,
    target_v,
    table_v,
    w1_v,
    x_v,
    metric_v,
    w23_v,
    w3t_v,
    response_v,
    tile_v,
    mask_v,
    anomaly_v,
    remap_v,
    w1t_v,
    adv_v,
    hid_v,
    tend_v,
    step_v,
    lay_v,
    q_v,
    updated_v,
    atmos_v,
    send_v,
    recv_v,
    near_send,
    near_recv,
    far_send,
    far_recv,
    in_sem,
    out_sem,
    lay_sem,
    send_sem,
    recv_sem,
    near_sem,
    far_sem,
):
    core, chip = lax.axis_index("sect"), lax.axis_index("dev")
    me = core * 64 + chip
    high, low = lax.div(me, 8), lax.rem(me, 8)
    x, y, z = lax.div(chip, 16), lax.rem(lax.div(chip, 4), 4), lax.rem(chip, 4)

    pairs = [
        (target_hbm.at[me], target_v),
        (table_hbm, table_v),
        (w1_hbm, w1_v),
        (state_hbm, x_v),
        (metric_hbm, metric_v),
        (w2t_hbm, w23_v.at[pl.ds(0, WIDTH)]),
        (w3t_hbm, w3t_v),
        (response_hbm, response_v),
        (tile_hbm, tile_v),
        (mask_hbm, mask_v),
        (anomaly_hbm, anomaly_v),
        (remap_hbm, remap_v),
    ]
    loads = [pltpu.make_async_copy(a, b, in_sem.at[i]) for i, (a, b) in enumerate(pairs)]
    for load in loads:
        load.start()

    cores = [lax.rem(core + k, 2) for k in range(2)]
    xs = [lax.rem(x + k, 4) * 16 for k in range(4)]
    ys = [lax.rem(y + k, 4) * 4 for k in range(4)]
    zs = [lax.rem(z + k, 4) for k in range(4)]
    barrier = pltpu.get_barrier_semaphore()
    for a, b, e, f in FAR_FIRST:
        if (a, b, e, f) != SELF:
            pl.semaphore_signal(barrier, inc=1, device_id=(cores[a], xs[b] + ys[e] + zs[f]), device_id_type=MESH)

    loads[0].wait()
    loads[1].wait()
    order = table_v[:, 256:384].astype(I32)
    to_device = (
        ((order[:, 0:1] + core) & 1) * 64
        + ((order[:, 1:2] + x) & 3) * 16
        + ((order[:, 2:3] + y) & 3) * 4
        + ((order[:, 3:4] + z) & 3)
    )

    targets = jnp.concatenate([target_v[k : k + 1, :] for k in range(8)], axis=1)
    before = one_hot(iota((STEP, STEP), 0) < iota((STEP, STEP), 1))
    message = iota((DEVICES, STEP), 0)
    taken = jnp.zeros((DEVICES, 1), F32)
    slots = []
    for c in range(COLS // STEP):
        hit = to_device == targets[:, c * STEP : (c + 1) * STEP]
        hits = jnp.where(hit, 1.0, 0.0)
        earlier = dot(hits.astype(BF16), before) + taken
        taken = taken + jnp.sum(hits, axis=1, keepdims=True)
        slot = jnp.where(hit, earlier.astype(I32) + CAP * message, 0)
        slots.append(jnp.sum(slot, axis=0, keepdims=True))
    slots = jnp.concatenate(slots, axis=1)

    loads[2].wait()
    unit = one_hot(iota((256, 256), 0) == iota((256, 256), 1))
    for b in range(HID // 256):
        rows = slice(b * 256, (b + 1) * 256)
        w1t_v[rows, :] = dot_nt(unit, w1_v[:, rows]).astype(BF16)

    for load in loads[3:8]:
        load.wait()
    w3t = w3t_v[...].astype(F32)
    w23_v[WIDTH : WIDTH + 16, :] = jnp.concatenate([w3t, jnp.zeros((12, HID), F32)], axis=0).astype(BF16)
    deriv = table_v[:, 0:256].astype(BF16)
    stores = []
    for c in range(COLS // STEP):
        for b in range(STEP // 128):
            at = slice(c * STEP + b * 128, c * STEP + (b + 1) * 128)
            field = x_v[:, at]
            grads = dot(field, deriv)
            wide = field.astype(F32)
            wind_first = wide[0:72] * metric_v[0:1, at]
            wind_second = wide[72:144] * metric_v[1:2, at]
            moved = (
                wide
                - jnp.concatenate([wind_first] * 4, axis=0) * grads[:, 0:128]
                - jnp.concatenate([wind_second] * 4, axis=0) * grads[:, 128:256]
            )
            adv_v[:, at] = moved.astype(BF16)
        at = slice(c * STEP, (c + 1) * STEP)
        column = adv_v[:, at]
        for b in range(HID // 256):
            rows = slice(b * 256, (b + 1) * 256)
            half = 0.5 * dot(w1t_v[rows, :], column)
            hid_v[rows, at] = (half + half * jnp.tanh(half)).astype(BF16)
        result = dot(w23_v[...], hid_v[:, at])
        tendency = result[0:WIDTH]
        step_v[:, at] = (column.astype(F32) + tendency).astype(BF16)
        tendency = tendency.astype(BF16)
        tend_v[0:WIDTH, at] = tendency
        for g in range(1, 4):
            tend_v[256 + 32 * g : 288 + 32 * g, at] = tendency[256:288]
        flux = result[WIDTH : WIDTH + 8].astype(BF16).astype(F32)
        mixed = sum(response_v[:, k : k + 1] * flux[k : k + 1] for k in range(4))
        for b in range(STEP // 128):
            j = c * (STEP // 128) + b
            q_v[j : j + 1, :] = mixed[:, b * 128 : (b + 1) * 128]
        store = pltpu.make_async_copy(step_v.at[:, at], stepped_out.at[:, at], out_sem.at[c])
        store.start()
        stores.append(store)

    for load in loads[8:]:
        load.wait()
    lane, sub = iota((8, 128), 1), iota((8, 128), 0)
    shift_row = jnp.where(iota((1, 128), 1) < 8, tile_v[0:1, :] >> 3, -1)
    shift_col = jnp.sum(jnp.where(lane == sub, shift_row, 0), axis=1, keepdims=True)
    same = jnp.where((shift_row == shift_col) & (lane < 8), 1, 0)
    twin_row = jnp.sum(jnp.where(sub < lane, same, 0), axis=0, keepdims=True)
    twin_col = jnp.sum(jnp.where(lane < sub, same, 0), axis=1, keepdims=True)

    ocean = mask_v[...].astype(F32)
    ahead = jnp.concatenate([ocean, ocean * anomaly_v[...]], axis=0).astype(BF16)
    near_send[...] = ahead
    near_recv[low] = ahead

    q = q_v[...]
    q_rows = jnp.concatenate([q, jnp.zeros((120, 128), F32)], axis=0).astype(BF16)
    flux_to = jnp.where(shift_row < 0, -1, (shift_row + me) & (DEVICES - 1))
    flux_rows = [dot(one_hot((to_device == flux_to) & (twin_row == u)), q_rows) for u in range(2)]

    pl.semaphore_wait(barrier, DEVICES - 1)

    for i in range(1, 8):
        pltpu.make_async_remote_copy(
            near_send,
            near_recv.at[low],
            near_sem.at[0],
            near_sem.at[1],
            device_id=device(high * 8 + lax.rem(low + i, 8)),
            device_id_type=MESH,
        ).start()

    plane = lax.div(me, 16)
    first = 0
    for k, count in enumerate(CHUNKS):
        size = count * CAP
        pick = one_hot(iota((size, COLS), 0) + first * CAP == slots)
        placed = dot_nt(pick, tend_v[...])
        into = pl.ds(first, count)
        main = placed[:, 0:256].astype(BF16)
        send_v[into, 0:16, :] = main[:, 0:128].reshape(count, CAP, 128)
        send_v[into, 16:32, :] = main[:, 128:256].reshape(count, CAP, 128)
        keep = (iota((size, 128), 0) & 15) >> 2 == iota((size, 128), 1) >> 5
        tail = jnp.where(keep, placed[:, 256:384], 0.0).reshape(count, CAP, 128)
        tail = tail[:, 0:8] + tail[:, 8:16]
        tail = tail + jnp.concatenate([tail[:, 4:8], tail[:, 0:4]], axis=1)
        packed_row = iota((count, 8, 128), 1)
        for u in range(2):
            row = flux_rows[u][first : first + count].reshape(count, 1, 128)
            tail = jnp.where(packed_row == 4 + u, row, tail)
        send_v[into, 32:40, :] = tail.astype(BF16)
        for i in range(first, first + count):
            a, b, e, f = ORDER[i]
            if ORDER[i] == SELF:
                pltpu.make_async_copy(send_v.at[i], recv_v.at[me], recv_sem.at[plane]).start()
                continue
            pltpu.make_async_remote_copy(
                send_v.at[i],
                recv_v.at[me],
                send_sem,
                recv_sem.at[plane],
                device_id=(cores[a], xs[b] + ys[e] + zs[f]),
                device_id_type=MESH,
            ).start()
        first += count
        if k == 2:
            got = near_recv.at[pl.ds(0, 7)]
            pltpu.make_async_copy(got, got, near_sem.at[1]).wait()
            source = (low + shift_col) & 7
            source = jnp.concatenate([source, source], axis=0)
            chosen = jnp.zeros((16, 128), F32)
            for l in range(8):
                chosen = chosen + jnp.where(source == l, near_recv[l].astype(F32), 0.0)
            chosen = chosen.astype(BF16)
            far_send[...] = chosen
            far_recv[high] = chosen
            for i in range(1, 16):
                pltpu.make_async_remote_copy(
                    far_send,
                    far_recv.at[high],
                    far_sem.at[0],
                    far_sem.at[1],
                    device_id=device(lax.rem(high + i, 16) * 8 + low),
                    device_id_type=MESH,
                ).start()

    slot, row = iota((256, 128), 0), iota((256, 128), 1)
    spread = one_hot((row >> 3 == slot >> 4) & ((row & 7) == (slot & 3)))
    held = (slot & 15) >> 2 == row >> 5
    fold = one_hot(iota((32, 128), 0) == (iota((32, 128), 1) & 31))
    flux_row = ((me - shift_col) & (DEVICES - 1)) * 8 + 4 + twin_col
    remap = remap_v[...]
    received = jnp.zeros((8, 128), F32)
    for quarter, planes in enumerate(QUARTERS):
        for a, b in planes:
            group = cores[a] * 4 + lax.rem(x - b + 4, 4)
            sixteen = pl.ds(pl.multiple_of(group * 16, 16), 16)
            got = recv_v.at[sixteen]
            pltpu.make_async_copy(got, got, recv_sem.at[group]).wait()
            lanes = pl.ds(pl.multiple_of(group * 256, 256), 256)
            main = jnp.concatenate(
                [recv_v[sixteen, 16 * h : 16 * h + 16, :].reshape(256, 128) for h in range(2)], axis=1
            )
            lay_v[0:256, lanes] = dot_nt(unit, main).astype(BF16)
            packed = recv_v[sixteen, 32:40, :].astype(F32).reshape(128, 128).astype(BF16)
            wide = jnp.where(held, dot(spread, packed), 0.0).astype(BF16)
            lay_v[256:288, lanes] = dot_nt(fold, wide).astype(BF16)
            received = received + dot(one_hot(iota((8, 128), 1) + group * 128 == flux_row), packed)
            pltpu.make_async_copy(lay_v.at[:, lanes], layout_out.at[:, lanes], lay_sem).start()
        if quarter == 2:
            got = far_recv.at[pl.ds(0, 15)]
            pltpu.make_async_copy(got, got, far_sem.at[1]).wait()
            source = ((me + shift_col) & (DEVICES - 1)) >> 3
            source = jnp.concatenate([source, source], axis=0)
            chosen = jnp.zeros((16, 128), F32)
            for h in range(16):
                chosen = chosen + jnp.where(source == h, far_recv[h].astype(F32), 0.0)
            cell = dot_nt(q, remap, lax.Precision.HIGHEST)
            masked = chosen[8:16] + chosen[0:8] * cell
            atmos_v[...] = jnp.dot(masked, remap, precision=lax.Precision.HIGHEST, preferred_element_type=F32)
            stores.append(pltpu.make_async_copy(atmos_v, atmos_out, out_sem.at[4]))
            stores[-1].start()

    cell = dot_nt(received, remap, lax.Precision.HIGHEST)
    updated_v[...] = anomaly_v[...] + mask_v[...].astype(F32) * cell
    stores.append(pltpu.make_async_copy(updated_v, updated_out, out_sem.at[5]))
    stores[-1].start()

    sent = send_v.at[pl.ds(0, DEVICES - 1)]
    pltpu.make_async_copy(sent, sent, send_sem).wait()
    sent = near_recv.at[pl.ds(0, 7)]
    pltpu.make_async_copy(sent, sent, near_sem.at[0]).wait()
    sent = far_recv.at[pl.ds(0, 15)]
    pltpu.make_async_copy(sent, sent, far_sem.at[0]).wait()
    for store in stores:
        store.wait()
    pltpu.make_async_copy(lay_v, layout_out, lay_sem).wait()


def hand_out(a, b, c, d, a_out, b_out, c_out, d_out, sem):
    copies = [
        pltpu.make_async_copy(source, result, sem.at[i])
        for i, (source, result) in enumerate(((b, b_out), (a, a_out), (c, c_out), (d, d_out)))
    ]
    for copy in copies:
        copy.start()
    for copy in copies:
        copy.wait()


def per_device(
    atmosphere_state,
    metric,
    column_group_target,
    physics_input_layer,
    physics_tendency_layer,
    physics_flux_layer,
    block_to_tile,
    remap_weight_matrix,
    ocean_land_mask,
    ocean_sea_anomaly,
    flux_sea_response,
):
    anywhere, hbm = pl.BlockSpec(memory_space=pl.ANY), pl.BlockSpec(memory_space=pltpu.HBM)
    results = [
        jax.ShapeDtypeStruct((WIDTH, COLS), BF16),
        jax.ShapeDtypeStruct((WIDTH, DEVICES * CAP), BF16),
        jax.ShapeDtypeStruct((8, 128), F32),
        jax.ShapeDtypeStruct((8, 128), F32),
    ]
    done = pl.pallas_call(
        kernel,
        out_shape=results,
        in_specs=[hbm] * 12,
        out_specs=[anywhere] * 4,
        scratch_shapes=[
            pltpu.VMEM((8, 128), I32),
            pltpu.VMEM((DEVICES, 384), F32),
            pltpu.VMEM((WIDTH, HID), BF16),
            pltpu.VMEM((WIDTH, COLS), BF16),
            pltpu.VMEM((2, COLS), F32),
            pltpu.VMEM((WIDTH + 16, HID), BF16),
            pltpu.VMEM((4, HID), BF16),
            pltpu.VMEM((1, 4), F32),
            pltpu.VMEM((8, 128), I32),
            pltpu.VMEM((8, 128), I32),
            pltpu.VMEM((8, 128), F32),
            pltpu.VMEM((128, 128), F32),
            pltpu.VMEM((HID, WIDTH), BF16),
            pltpu.VMEM((WIDTH, COLS), BF16),
            pltpu.VMEM((HID, COLS), BF16),
            pltpu.VMEM((384, COLS), BF16),
            pltpu.VMEM((WIDTH, COLS), BF16),
            pltpu.VMEM((WIDTH, DEVICES * CAP), BF16),
            pltpu.VMEM((8, 128), F32),
            pltpu.VMEM((8, 128), F32),
            pltpu.VMEM((8, 128), F32),
            pltpu.VMEM((DEVICES, ROWS, 128), BF16),
            pltpu.VMEM((DEVICES, ROWS, 128), BF16),
            pltpu.VMEM((16, 128), BF16),
            pltpu.VMEM((8, 16, 128), BF16),
            pltpu.VMEM((16, 128), BF16),
            pltpu.VMEM((16, 16, 128), BF16),
            pltpu.SemaphoreType.DMA((12,)),
            pltpu.SemaphoreType.DMA((6,)),
            pltpu.SemaphoreType.DMA,
            pltpu.SemaphoreType.DMA,
            pltpu.SemaphoreType.DMA((8,)),
            pltpu.SemaphoreType.DMA((2,)),
            pltpu.SemaphoreType.DMA((2,)),
        ],
        compiler_params=pltpu.CompilerParams(
            collective_id=0, has_side_effects=True, vmem_limit_bytes=VMEM_LIMIT
        ),
        name="coupling_interval",
    )(*[pltpu.with_memory_space_constraint(v, pltpu.HBM) for v in (
        column_group_target.reshape(DEVICES, 8, 128),
        jnp.asarray(tables()),
        physics_input_layer,
        atmosphere_state.reshape(WIDTH, COLS),
        metric,
        physics_tendency_layer.T,
        physics_flux_layer.T,
        flux_sea_response.reshape(1, 4),
        block_to_tile.reshape(8, 128),
        ocean_land_mask,
        ocean_sea_anomaly,
        remap_weight_matrix,
    )])
    stepped, layout, updated, atmos = pl.pallas_call(
        hand_out,
        out_shape=results,
        in_specs=[anywhere] * 4,
        out_specs=[anywhere] * 4,
        scratch_shapes=[pltpu.SemaphoreType.DMA((4,))],
        compiler_params=pltpu.CompilerParams(vmem_limit_bytes=4 * 1024 * 1024),
        name="hand_out",
    )(*done)
    return (
        stepped.reshape(atmosphere_state.shape),
        layout.T,
        updated,
        atmos.reshape(COLS),
    )


def solution(mesh):
    placed = (
        P(None, None, ("sect", "dev")),
        P(None, ("sect", "dev")),
        P(),
        P(),
        P(),
        P(),
        P(),
        P(),
        P(("sect", "dev"), None),
        P(("sect", "dev"), None),
        P(),
    )
    return jax.shard_map(
        per_device,
        mesh=mesh,
        in_specs=placed,
        out_specs=(
            P(None, None, ("sect", "dev")),
            P(("sect", "dev"), None),
            P(("sect", "dev"), None),
            P(("sect", "dev")),
        ),
        check_vma=False,
    )
```

```python
import functools
import itertools
import random

import jax
import jax.numpy as jnp
import numpy as np
from jax import lax
from jax.experimental import pallas as pl
from jax.experimental.pallas import tpu as pltpu
from jax.sharding import PartitionSpec as P

MESH = pl.DeviceIdType.MESH
BF16 = jnp.bfloat16
F32 = jnp.float32
I32 = jnp.int32

DEVICES = 128
CAP = 16
COLS = 1024
WIDTH = 288
HID = 1024
ROWS = 40
STEP = 256
WIDE = 512
VMEM_LIMIT = 32 * 1024 * 1024
NT = (((1,), (1,)), ((), ()))


def gll_tables():
    gll_nodes = np.array([-1.0, -1.0 / np.sqrt(5.0), 1.0 / np.sqrt(5.0), 1.0])
    offdiag = gll_nodes[:, None] - gll_nodes[None, :] + np.eye(4)
    bary = np.prod(offdiag, axis=1)
    derivative = bary[:, None] / (bary[None, :] * offdiag)
    diag_sum = np.sum(1.0 / offdiag - np.eye(4), axis=1)
    derivative = derivative * (1.0 - np.eye(4)) + np.eye(4) * diag_sum[:, None]
    first_dir = np.kron(np.eye(8), np.kron(np.eye(4), derivative)).T
    second_dir = np.kron(np.eye(8), np.kron(derivative, np.eye(4))).T
    return np.concatenate([first_dir, second_dir], axis=1)


QUARTERS = [[(0, 1), (0, 3)], [(1, 1), (1, 3)], [(0, 2), (0, 0)], [(1, 2), (1, 0)]]


def message_order():
    hops = lambda k: min(k, 4 - k)
    mixed, order = random.Random(1), []
    for planes in QUARTERS:
        part = [plane + yz for plane in planes for yz in itertools.product(range(4), range(4))]
        mixed.shuffle(part)
        part.sort(key=lambda o: (o == SELF, -sum(hops(k) for k in o[1:])))
        order += part
    return order


SELF = (0, 0, 0, 0)
ORDER = message_order()
FAR_FIRST = sorted(ORDER, key=lambda o: -sum(min(k, 4 - k) for k in o[1:]))
CHUNKS = [8, 24, 32, 32, 32]


def tables():
    table = np.zeros((DEVICES, 384), np.float32)
    table[:, :256] = gll_tables()
    table[:, 256:260] = ORDER
    return table


def device(index):
    return (lax.div(index, 64), lax.rem(index, 64))


def dot(a, b):
    return jnp.dot(a, b, preferred_element_type=F32)


def dot_nt(a, b, precision=None):
    return lax.dot_general(a, b, NT, precision=precision, preferred_element_type=F32)


def iota(shape, dim):
    return lax.broadcasted_iota(I32, shape, dim)


def one_hot(condition):
    return jnp.where(condition, 1.0, 0.0).astype(BF16)


def kernel(
    target_hbm,
    table_hbm,
    w1_hbm,
    state_hbm,
    metric_hbm,
    w2t_hbm,
    w3t_hbm,
    response_hbm,
    tile_hbm,
    mask_hbm,
    anomaly_hbm,
    remap_hbm,
    stepped_out,
    layout_out,
    updated_out,
    atmos_out,
    target_v,
    table_v,
    w1_v,
    x_v,
    metric_v,
    w23_v,
    w3t_v,
    response_v,
    tile_v,
    mask_v,
    anomaly_v,
    remap_v,
    w1t_v,
    adv_v,
    hid_v,
    tend_v,
    q_v,
    send_v,
    recv_v,
    ahead_send,
    ahead_recv,
    in_sem,
    send_sem,
    recv_sem,
    ahead_sent,
    ahead_sem,
):
    core, chip = lax.axis_index("sect"), lax.axis_index("dev")
    me = core * 64 + chip
    x, y, z = lax.div(chip, 16), lax.rem(lax.div(chip, 4), 4), lax.rem(chip, 4)

    half = COLS // 2
    pairs = [
        (state_hbm.at[:, pl.ds(0, half)], x_v.at[:, pl.ds(0, half)]),
        (state_hbm.at[:, pl.ds(half, half)], x_v.at[:, pl.ds(half, half)]),
        (metric_hbm, metric_v),
        (table_hbm, table_v),
        (w1_hbm.at[:, pl.ds(0, half)], w1_v.at[:, pl.ds(0, half)]),
        (w1_hbm.at[:, pl.ds(half, half)], w1_v.at[:, pl.ds(half, half)]),
        (target_hbm.at[me], target_v),
        (w2t_hbm.at[:, pl.ds(0, half)], w23_v.at[pl.ds(0, WIDTH), pl.ds(0, half)]),
        (w2t_hbm.at[:, pl.ds(half, half)], w23_v.at[pl.ds(0, WIDTH), pl.ds(half, half)]),
        (w3t_hbm, w3t_v),
        (response_hbm, response_v),
        (tile_hbm, tile_v),
        (mask_hbm, mask_v),
        (anomaly_hbm, anomaly_v),
        (remap_hbm, remap_v),
    ]
    loads = [pltpu.make_async_copy(a, b, in_sem.at[i]) for i, (a, b) in enumerate(pairs)]
    for load in loads:
        load.start()

    cores = [lax.rem(core + k, 2) for k in range(2)]
    xs = [lax.rem(x + k, 4) * 16 for k in range(4)]
    ys = [lax.rem(y + k, 4) * 4 for k in range(4)]
    zs = [lax.rem(z + k, 4) for k in range(4)]
    barrier = pltpu.get_barrier_semaphore()
    for a, b, e, f in FAR_FIRST:
        if (a, b, e, f) != SELF:
            pl.semaphore_signal(barrier, inc=1, device_id=(cores[a], xs[b] + ys[e] + zs[f]), device_id_type=MESH)

    for load in loads[0:4]:
        load.wait()
    deriv = table_v[:, 0:256].astype(BF16)

    def dynamics(b):
        at = slice(b * 128, (b + 1) * 128)
        field = x_v[:, at]
        grads = dot(field, deriv)
        wide = field.astype(F32)
        wind_first = wide[0:72] * metric_v[0:1, at]
        wind_second = wide[72:144] * metric_v[1:2, at]
        moved = (
            wide
            - jnp.concatenate([wind_first] * 4, axis=0) * grads[:, 0:128]
            - jnp.concatenate([wind_second] * 4, axis=0) * grads[:, 128:256]
        )
        adv_v[:, at] = moved.astype(BF16)

    def first_layer(c, b):
        at, rows = slice(c * WIDE, (c + 1) * WIDE), slice(b * 256, (b + 1) * 256)
        half = 0.5 * dot(w1t_v[rows, :], adv_v[:, at])
        hid_v[rows, at] = (half + half * jnp.tanh(half)).astype(BF16)

    def second_layer(c):
        at = slice(c * WIDE, (c + 1) * WIDE)
        result = dot(w23_v[...], hid_v[:, at])
        tendency = result[0:WIDTH]
        stepped_out[:, at] = (adv_v[:, at].astype(F32) + tendency).astype(BF16)
        tendency = tendency.astype(BF16)
        tend_v[0:WIDTH, at] = tendency
        for g in range(1, 4):
            tend_v[256 + 32 * g : 288 + 32 * g, at] = tendency[256:288]
        flux = result[WIDTH : WIDTH + 8].astype(BF16).astype(F32)
        mixed = sum(response_v[:, k : k + 1] * flux[k : k + 1] for k in range(4))
        for b in range(WIDE // 128):
            j = c * (WIDE // 128) + b
            q_v[j : j + 1, :] = mixed[:, b * 128 : (b + 1) * 128]

    for b in range(WIDE // 128):
        dynamics(b)

    for load in loads[4:7]:
        load.wait()
    unit = one_hot(iota((256, 256), 0) == iota((256, 256), 1))
    for b in range(HID // 256):
        rows = slice(b * 256, (b + 1) * 256)
        w1t_v[rows, :] = dot_nt(unit, w1_v[:, rows]).astype(BF16)

    for c in range(COLS // WIDE):
        for b in range(HID // 256):
            first_layer(c, b)
            if c + 1 < COLS // WIDE:
                for d in range(WIDE // 512):
                    dynamics((c + 1) * WIDE // 128 + b * (WIDE // 512) + d)
        if c == 0:
            for load in loads[7:]:
                load.wait()
            w3t = w3t_v[...].astype(F32)
            w23_v[WIDTH : WIDTH + 16, :] = jnp.concatenate([w3t, jnp.zeros((12, HID), F32)], axis=0).astype(BF16)
        else:
            second_layer(c - 1)
    order = table_v[:, 256:384].astype(I32)
    to_device = (
        ((order[:, 0:1] + core) & 1) * 64
        + ((order[:, 1:2] + x) & 3) * 16
        + ((order[:, 2:3] + y) & 3) * 4
        + ((order[:, 3:4] + z) & 3)
    )

    targets = jnp.concatenate([target_v[k : k + 1, :] for k in range(8)], axis=1)
    before = one_hot(iota((STEP, STEP), 0) < iota((STEP, STEP), 1))
    message = iota((DEVICES, STEP), 0)
    taken = jnp.zeros((DEVICES, 1), F32)
    slots = []
    for c in range(COLS // STEP):
        hit = to_device == targets[:, c * STEP : (c + 1) * STEP]
        hits = jnp.where(hit, 1.0, 0.0)
        earlier = dot(hits.astype(BF16), before) + taken
        taken = taken + jnp.sum(hits, axis=1, keepdims=True)
        slot = jnp.where(hit, earlier.astype(I32) + CAP * message, 0)
        slots.append(jnp.sum(slot, axis=0, keepdims=True))
    slots = jnp.concatenate(slots, axis=1)

    second_layer(COLS // WIDE - 1)

    lane, sub = iota((8, 128), 1), iota((8, 128), 0)
    shift_row = jnp.where(iota((1, 128), 1) < 8, tile_v[0:1, :] >> 3, -1)
    shift_col = jnp.sum(jnp.where(lane == sub, shift_row, 0), axis=1, keepdims=True)
    same = jnp.where((shift_row == shift_col) & (lane < 8), 1, 0)
    twin_row = jnp.sum(jnp.where(sub < lane, same, 0), axis=0, keepdims=True)
    twin_col = jnp.sum(jnp.where(lane < sub, same, 0), axis=1, keepdims=True)

    ocean = mask_v[...].astype(F32)
    ahead = jnp.concatenate([ocean, ocean * anomaly_v[...]], axis=0).astype(BF16)
    tile_device = (me + jnp.concatenate([shift_col, shift_col], axis=0)) & (DEVICES - 1)
    plane = lax.div(me, 16)
    steps = [
        (4, z, tile_device & 3, lambda k: plane * 16 + y * 4 + k),
        (4, y, (tile_device >> 2) & 3, lambda k: plane * 16 + k * 4 + z),
        (8, plane, tile_device >> 4, lambda k: k * 16 + y * 4 + z),
    ]

    def ocean_send(n, rows):
        size, mine, _, peer = steps[n]
        ahead_send[n] = rows
        ahead_recv[4 * n + mine] = rows
        for k in range(1, size):
            pltpu.make_async_remote_copy(
                ahead_send.at[n],
                ahead_recv.at[4 * n + mine],
                ahead_sent.at[n],
                ahead_sem.at[n],
                device_id=device(peer(lax.rem(mine + k, size))),
                device_id_type=MESH,
            ).start()

    def ocean_receive(n):
        size, _, source, _ = steps[n]
        got = ahead_recv.at[pl.ds(4 * n, size - 1)]
        pltpu.make_async_copy(got, got, ahead_sem.at[n]).wait()
        chosen = jnp.zeros((16, 128), F32)
        for k in range(size):
            chosen = chosen + jnp.where(source == k, ahead_recv[4 * n + k].astype(F32), 0.0)
        return chosen

    remap = remap_v[...]
    cell = dot_nt(q_v[...], remap, lax.Precision.HIGHEST)
    cell_rows = jnp.concatenate([cell, jnp.zeros((120, 128), F32)], axis=0).astype(BF16)
    cell_to = jnp.where(shift_row < 0, -1, (shift_row + me) & (DEVICES - 1))
    cell_rows = [dot(one_hot((to_device == cell_to) & (twin_row == u)), cell_rows) for u in range(2)]

    pl.semaphore_wait(barrier, DEVICES - 1)

    ocean_send(0, ahead)

    first = 0
    for k, count in enumerate(CHUNKS):
        size = count * CAP
        pick = one_hot(iota((size, COLS), 0) + first * CAP == slots)
        placed = dot_nt(pick, tend_v[...])
        into = pl.ds(first, count)
        main = placed[:, 0:256].astype(BF16)
        send_v[into, 0:16, :] = main[:, 0:128].reshape(count, CAP, 128)
        send_v[into, 16:32, :] = main[:, 128:256].reshape(count, CAP, 128)
        keep = (iota((size, 128), 0) & 15) >> 2 == iota((size, 128), 1) >> 5
        tail = jnp.where(keep, placed[:, 256:384], 0.0).reshape(count, CAP, 128)
        tail = tail[:, 0:8] + tail[:, 8:16]
        tail = tail + jnp.concatenate([tail[:, 4:8], tail[:, 0:4]], axis=1)
        packed_row = iota((count, 8, 128), 1)
        for u in range(2):
            row = cell_rows[u][first : first + count].reshape(count, 1, 128)
            tail = jnp.where(packed_row == 4 + u, row, tail)
        send_v[into, 32:40, :] = tail.astype(BF16)
        for i in range(first, first + count):
            a, b, e, f = ORDER[i]
            if ORDER[i] == SELF:
                pltpu.make_async_copy(send_v.at[i], recv_v.at[me], recv_sem.at[plane]).start()
                continue
            pltpu.make_async_remote_copy(
                send_v.at[i],
                recv_v.at[me],
                send_sem,
                recv_sem.at[plane],
                device_id=(cores[a], xs[b] + ys[e] + zs[f]),
                device_id_type=MESH,
            ).start()
        first += count
        if k in (2, 3):
            ocean_send(k - 1, ocean_receive(k - 2).astype(BF16))

    slot, row = iota((256, 128), 0), iota((256, 128), 1)
    spread = one_hot((row >> 3 == slot >> 4) & ((row & 7) == (slot & 3)))
    held = (slot & 15) >> 2 == row >> 5
    fold = one_hot(iota((32, 128), 0) == (iota((32, 128), 1) & 31))
    cell_row = ((me - shift_col) & (DEVICES - 1)) * 8 + 4 + twin_col
    received = jnp.zeros((8, 128), F32)
    for quarter, planes in enumerate(QUARTERS):
        groups = [cores[a] * 4 + lax.rem(x - b + 4, 4) for a, b in planes]
        for group in groups:
            got = recv_v.at[pl.ds(pl.multiple_of(group * 16, 16), 16)]
            pltpu.make_async_copy(got, got, recv_sem.at[group]).wait()
        for group in groups:
            sixteen = pl.ds(pl.multiple_of(group * 16, 16), 16)
            lanes = pl.ds(pl.multiple_of(group * 256, 256), 256)
            main = jnp.concatenate(
                [recv_v[sixteen, 16 * h : 16 * h + 16, :].reshape(256, 128) for h in range(2)], axis=1
            )
            layout_out[0:256, lanes] = dot_nt(unit, main).astype(BF16)
            packed = recv_v[sixteen, 32:40, :].astype(F32).reshape(128, 128).astype(BF16)
            wide = jnp.where(held, dot(spread, packed), 0.0).astype(BF16)
            layout_out[256:288, lanes] = dot_nt(fold, wide).astype(BF16)
            received = received + dot(one_hot(iota((8, 128), 1) + group * 128 == cell_row), packed)
        if quarter == 2:
            chosen = ocean_receive(2)
            masked = chosen[8:16] + chosen[0:8] * cell
            atmos_out[...] = jnp.dot(masked, remap, precision=lax.Precision.HIGHEST, preferred_element_type=F32)
    updated_out[...] = anomaly_v[...] + mask_v[...].astype(F32) * received

    sent = send_v.at[pl.ds(0, DEVICES - 1)]
    pltpu.make_async_copy(sent, sent, send_sem).wait()
    for n, (size, _, _, _) in enumerate(steps):
        sent = ahead_recv.at[pl.ds(4 * n, size - 1)]
        pltpu.make_async_copy(sent, sent, ahead_sent.at[n]).wait()


def hand_out(a, b, c, d, a_out, b_out, c_out, d_out, sem):
    pieces = [(b.at[rows], b_out.at[rows]) for rows in (pl.ds(k * 72, 72) for k in range(4))]
    pieces += [(a.at[rows], a_out.at[rows]) for rows in (pl.ds(k * 144, 144) for k in range(2))]
    pieces += [(c, c_out), (d, d_out)]
    copies = [pltpu.make_async_copy(source, result, sem.at[i]) for i, (source, result) in enumerate(pieces)]
    for copy in copies:
        copy.start()
    for copy in copies:
        copy.wait()


def per_device(
    atmosphere_state,
    metric,
    column_group_target,
    physics_input_layer,
    physics_tendency_layer,
    physics_flux_layer,
    block_to_tile,
    remap_weight_matrix,
    ocean_land_mask,
    ocean_sea_anomaly,
    flux_sea_response,
):
    anywhere, vmem, hbm = (pl.BlockSpec(memory_space=space) for space in (pl.ANY, pltpu.VMEM, pltpu.HBM))
    results = [
        jax.ShapeDtypeStruct((WIDTH, COLS), BF16),
        jax.ShapeDtypeStruct((WIDTH, DEVICES * CAP), BF16),
        jax.ShapeDtypeStruct((8, 128), F32),
        jax.ShapeDtypeStruct((8, 128), F32),
    ]
    done = pl.pallas_call(
        kernel,
        out_shape=results,
        in_specs=[hbm] * 12,
        out_specs=[vmem] * 4,
        scratch_shapes=[
            pltpu.VMEM((8, 128), I32),
            pltpu.VMEM((DEVICES, 384), F32),
            pltpu.VMEM((WIDTH, HID), BF16),
            pltpu.VMEM((WIDTH, COLS), BF16),
            pltpu.VMEM((2, COLS), F32),
            pltpu.VMEM((WIDTH + 16, HID), BF16),
            pltpu.VMEM((4, HID), BF16),
            pltpu.VMEM((1, 4), F32),
            pltpu.VMEM((8, 128), I32),
            pltpu.VMEM((8, 128), I32),
            pltpu.VMEM((8, 128), F32),
            pltpu.VMEM((128, 128), F32),
            pltpu.VMEM((HID, WIDTH), BF16),
            pltpu.VMEM((WIDTH, COLS), BF16),
            pltpu.VMEM((HID, COLS), BF16),
            pltpu.VMEM((384, COLS), BF16),
            pltpu.VMEM((8, 128), F32),
            pltpu.VMEM((DEVICES, ROWS, 128), BF16),
            pltpu.VMEM((DEVICES, ROWS, 128), BF16),
            pltpu.VMEM((3, 16, 128), BF16),
            pltpu.VMEM((16, 16, 128), BF16),
            pltpu.SemaphoreType.DMA((15,)),
            pltpu.SemaphoreType.DMA,
            pltpu.SemaphoreType.DMA((8,)),
            pltpu.SemaphoreType.DMA((3,)),
            pltpu.SemaphoreType.DMA((3,)),
        ],
        compiler_params=pltpu.CompilerParams(
            collective_id=0, has_side_effects=True, vmem_limit_bytes=VMEM_LIMIT
        ),
        name="coupling_interval",
    )(*[pltpu.with_memory_space_constraint(v, pltpu.HBM) for v in (
        column_group_target.reshape(DEVICES, 8, 128),
        jnp.asarray(tables()),
        physics_input_layer,
        atmosphere_state.reshape(WIDTH, COLS),
        metric,
        physics_tendency_layer.T,
        physics_flux_layer.T,
        flux_sea_response.reshape(1, 4),
        block_to_tile.reshape(8, 128),
        ocean_land_mask,
        ocean_sea_anomaly,
        remap_weight_matrix,
    )])
    stepped, layout, updated, atmos = pl.pallas_call(
        hand_out,
        out_shape=results,
        in_specs=[anywhere] * 4,
        out_specs=[anywhere] * 4,
        scratch_shapes=[pltpu.SemaphoreType.DMA((8,))],
        compiler_params=pltpu.CompilerParams(vmem_limit_bytes=4 * 1024 * 1024),
        name="hand_out",
    )(*done)
    return (
        stepped.reshape(atmosphere_state.shape),
        layout.T,
        updated,
        atmos.reshape(COLS),
    )


def solution(mesh):
    placed = (
        P(None, None, ("sect", "dev")),
        P(None, ("sect", "dev")),
        P(),
        P(),
        P(),
        P(),
        P(),
        P(),
        P(("sect", "dev"), None),
        P(("sect", "dev"), None),
        P(),
    )
    return jax.shard_map(
        per_device,
        mesh=mesh,
        in_specs=placed,
        out_specs=(
            P(None, None, ("sect", "dev")),
            P(("sect", "dev"), None),
            P(("sect", "dev"), None),
            P(("sect", "dev")),
        ),
        check_vma=False,
    )
```

```python
import functools
import itertools
import random

import jax
import jax.numpy as jnp
import numpy as np
from jax import lax
from jax.experimental import pallas as pl
from jax.experimental.pallas import tpu as pltpu
from jax.sharding import PartitionSpec as P

MESH = pl.DeviceIdType.MESH
BF16 = jnp.bfloat16
F32 = jnp.float32
I32 = jnp.int32

DEVICES = 128
CAP = 16
COLS = 1024
WIDTH = 288
HID = 1024
ROWS = 9
STEP = 256
WIDE = 512
EARLY = 5
VMEM_LIMIT = 32 * 1024 * 1024
NT = (((1,), (1,)), ((), ()))


def gll_tables():
    gll_nodes = np.array([-1.0, -1.0 / np.sqrt(5.0), 1.0 / np.sqrt(5.0), 1.0])
    offdiag = gll_nodes[:, None] - gll_nodes[None, :] + np.eye(4)
    bary = np.prod(offdiag, axis=1)
    derivative = bary[:, None] / (bary[None, :] * offdiag)
    diag_sum = np.sum(1.0 / offdiag - np.eye(4), axis=1)
    derivative = derivative * (1.0 - np.eye(4)) + np.eye(4) * diag_sum[:, None]
    first_dir = np.kron(np.eye(8), np.kron(np.eye(4), derivative)).T
    second_dir = np.kron(np.eye(8), np.kron(derivative, np.eye(4))).T
    return np.concatenate([first_dir, second_dir], axis=1)


QUARTERS = [[(0, 1), (0, 3)], [(1, 1), (1, 3)], [(0, 2), (0, 0)], [(1, 2), (1, 0)]]


def message_order():
    hops = lambda k: min(k, 4 - k)
    mixed, order = random.Random(1), []
    for planes in QUARTERS:
        part = [plane + yz for plane in planes for yz in itertools.product(range(4), range(4))]
        mixed.shuffle(part)
        part.sort(key=lambda o: (o == SELF, -sum(hops(k) for k in o[1:])))
        order += part
    return order


SELF = (0, 0, 0, 0)
ORDER = message_order()
FAR_FIRST = sorted(ORDER, key=lambda o: -sum(min(k, 4 - k) for k in o[1:]))
DIRECT = [16, 16]
CHUNKS = [32, 32, 32]


def tables():
    table = np.zeros((DEVICES, 384), np.float32)
    table[:, :256] = gll_tables()
    table[:, 256:260] = ORDER
    return table


def device(index):
    return (lax.div(index, 64), lax.rem(index, 64))


def dot(a, b):
    return jnp.dot(a, b, preferred_element_type=F32)


def dot_nt(a, b, precision=None):
    return lax.dot_general(a, b, NT, precision=precision, preferred_element_type=F32)


def iota(shape, dim):
    return lax.broadcasted_iota(I32, shape, dim)


def one_hot(condition):
    return jnp.where(condition, 1.0, 0.0).astype(BF16)


def kernel(
    target_hbm,
    table_hbm,
    w1_hbm,
    state_hbm,
    metric_hbm,
    w2t_hbm,
    w3t_hbm,
    response_hbm,
    tile_hbm,
    mask_hbm,
    anomaly_hbm,
    remap_hbm,
    stepped_out,
    layout_out,
    updated_out,
    atmos_out,
    target_v,
    table_v,
    w1_v,
    x_v,
    metric_v,
    w23_v,
    w3t_v,
    response_v,
    tile_v,
    mask_v,
    anomaly_v,
    remap_v,
    w1t_v,
    adv_v,
    hid_v,
    tend_v,
    q_v,
    send_v,
    recv_v,
    ocean_out,
    ocean_in,
    cell_out,
    cell_in,
    in_sem,
    send_sem,
    recv_sem,
    ocean_sent,
    ocean_came,
    cell_sent,
    cell_came,
):
    core, chip = lax.axis_index("sect"), lax.axis_index("dev")
    me = core * 64 + chip
    x, y, z = lax.div(chip, 16), lax.rem(lax.div(chip, 4), 4), lax.rem(chip, 4)

    half = COLS // 2
    pairs = [
        (target_hbm.at[me], target_v),
        (table_hbm, table_v),
        (metric_hbm, metric_v),
        (state_hbm.at[:, pl.ds(0, half)], x_v.at[:, pl.ds(0, half)]),
        (state_hbm.at[:, pl.ds(half, half)], x_v.at[:, pl.ds(half, half)]),
        (w1_hbm.at[:, pl.ds(0, half)], w1_v.at[:, pl.ds(0, half)]),
        (w1_hbm.at[:, pl.ds(half, half)], w1_v.at[:, pl.ds(half, half)]),
        (w2t_hbm.at[:, pl.ds(0, half)], w23_v.at[pl.ds(0, WIDTH), pl.ds(0, half)]),
        (w2t_hbm.at[:, pl.ds(half, half)], w23_v.at[pl.ds(0, WIDTH), pl.ds(half, half)]),
        (w3t_hbm, w3t_v),
        (response_hbm, response_v),
        (tile_hbm, tile_v),
        (mask_hbm, mask_v),
        (anomaly_hbm, anomaly_v),
        (remap_hbm, remap_v),
    ]
    loads = [pltpu.make_async_copy(a, b, in_sem.at[i]) for i, (a, b) in enumerate(pairs)]
    for load in loads:
        load.start()

    cores = [lax.rem(core + k, 2) for k in range(2)]
    xs = [lax.rem(x + k, 4) * 16 for k in range(4)]
    ys = [lax.rem(y + k, 4) * 4 for k in range(4)]
    zs = [lax.rem(z + k, 4) for k in range(4)]
    barrier = pltpu.get_barrier_semaphore()
    for a, b, e, f in FAR_FIRST:
        if (a, b, e, f) != SELF:
            pl.semaphore_signal(barrier, inc=1, device_id=(cores[a], xs[b] + ys[e] + zs[f]), device_id_type=MESH)

    for load in loads[0:5]:
        load.wait()
    deriv = table_v[:, 0:256].astype(BF16)

    def dynamics(b):
        at = slice(b * 128, (b + 1) * 128)
        field = x_v[:, at]
        grads = dot(field, deriv)
        wide = field.astype(F32)
        wind_first = wide[0:72] * metric_v[0:1, at]
        wind_second = wide[72:144] * metric_v[1:2, at]
        moved = (
            wide
            - jnp.concatenate([wind_first] * 4, axis=0) * grads[:, 0:128]
            - jnp.concatenate([wind_second] * 4, axis=0) * grads[:, 128:256]
        )
        adv_v[:, at] = moved.astype(BF16)

    def first_layer(c, b):
        at, rows = slice(c * WIDE, (c + 1) * WIDE), slice(b * 256, (b + 1) * 256)
        half = 0.5 * dot(w1t_v[rows, :], adv_v[:, at])
        hid_v[rows, at] = (half + half * jnp.tanh(half)).astype(BF16)

    def second_layer(c):
        at = slice(c * WIDE, (c + 1) * WIDE)
        result = dot(w23_v[...], hid_v[:, at])
        tendency = result[0:WIDTH]
        stepped_out[:, at] = (adv_v[:, at].astype(F32) + tendency).astype(BF16)
        tendency = tendency.astype(BF16)
        tend_v[0:WIDTH, at] = tendency
        for g in range(1, 4):
            tend_v[256 + 32 * g : 288 + 32 * g, at] = tendency[256:288]
        flux = result[WIDTH : WIDTH + 8].astype(BF16).astype(F32)
        mixed = sum(response_v[:, k : k + 1] * flux[k : k + 1] for k in range(4))
        for b in range(WIDE // 128):
            j = c * (WIDE // 128) + b
            q_v[j : j + 1, :] = mixed[:, b * 128 : (b + 1) * 128]

    for b in range(COLS // 128):
        dynamics(b)

    order = table_v[:, 256:384].astype(I32)
    to_device = (
        ((order[:, 0:1] + core) & 1) * 64
        + ((order[:, 1:2] + x) & 3) * 16
        + ((order[:, 2:3] + y) & 3) * 4
        + ((order[:, 3:4] + z) & 3)
    )

    targets = jnp.concatenate([target_v[k : k + 1, :] for k in range(8)], axis=1)
    before = one_hot(iota((STEP, STEP), 0) < iota((STEP, STEP), 1))
    message = iota((DEVICES, STEP), 0)
    taken = jnp.zeros((DEVICES, 1), F32)
    slots = []
    for c in range(COLS // STEP):
        hit = to_device == targets[:, c * STEP : (c + 1) * STEP]
        hits = jnp.where(hit, 1.0, 0.0)
        earlier = dot(hits.astype(BF16), before) + taken
        taken = taken + jnp.sum(hits, axis=1, keepdims=True)
        slot = jnp.where(hit, earlier.astype(I32) + CAP * message, 0)
        slots.append(jnp.sum(slot, axis=0, keepdims=True))
    slots = jnp.concatenate(slots, axis=1)

    plane = lax.div(me, 16)

    def lay_out(first, count, main, tail):
        size, into = count * CAP, pl.ds(first, count)
        main = main.astype(BF16)
        send_v[into, 0:4] = main[:, 0:128].reshape(count, 4, 4, 128)
        send_v[into, 4:8] = main[:, 128:256].reshape(count, 4, 4, 128)
        keep = (iota((size, 128), 0) & 15) >> 2 == iota((size, 128), 1) >> 5
        tail = jnp.where(keep, tail, 0.0).reshape(count, CAP, 128)
        tail = tail[:, 0:8] + tail[:, 8:16]
        send_v[into, 8] = (tail[:, 0:4] + tail[:, 4:8]).astype(BF16)

    def issue(first, count):
        for i in range(first, first + count):
            a, b, e, f = ORDER[i]
            if ORDER[i] == SELF:
                pltpu.make_async_copy(send_v.at[i], recv_v.at[me], recv_sem.at[plane]).start()
                continue
            pltpu.make_async_remote_copy(
                send_v.at[i],
                recv_v.at[me],
                send_sem,
                recv_sem.at[plane],
                device_id=(cores[a], xs[b] + ys[e] + zs[f]),
                device_id_type=MESH,
            ).start()

    def pick(first, count):
        return one_hot(iota((count * CAP, COLS), 0) + first * CAP == slots)

    for load in loads[5:]:
        load.wait()
    lane, sub = iota((8, 128), 1), iota((8, 128), 0)
    shift_row = jnp.where(iota((1, 128), 1) < 8, tile_v[0:1, :] >> 3, -1)
    shift_col = jnp.sum(jnp.where(lane == sub, shift_row, 0), axis=1, keepdims=True)

    def steps(devices):
        return [
            (4, z, devices & 3, lambda k: plane * 16 + y * 4 + k),
            (4, y, (devices >> 2) & 3, lambda k: plane * 16 + k * 4 + z),
            (8, plane, devices >> 4, lambda k: k * 16 + y * 4 + z),
        ]

    def pass_on(way, n, rows):
        (moves, out_v, in_v, sent, came) = way
        size, mine, _, peer = moves[n]
        out_v[n] = rows
        in_v[4 * n + mine] = rows
        for k in range(1, size):
            pltpu.make_async_remote_copy(
                out_v.at[n],
                in_v.at[4 * n + mine],
                sent.at[n],
                came.at[n],
                device_id=device(peer(lax.rem(mine + k, size))),
                device_id_type=MESH,
            ).start()

    def take(way, n):
        (moves, _, in_v, _, came) = way
        size, _, source, _ = moves[n]
        got = in_v.at[pl.ds(4 * n, size - 1)]
        pltpu.make_async_copy(got, got, came.at[n]).wait()
        chosen = jnp.zeros(in_v.shape[1:], F32)
        for k in range(size):
            chosen = chosen + jnp.where(source == k, in_v[4 * n + k].astype(F32), 0.0)
        return chosen

    tile_device = (me + jnp.concatenate([shift_col, shift_col], axis=0)) & (DEVICES - 1)
    block_device = (me - shift_col) & (DEVICES - 1)
    to_block = (steps(tile_device), ocean_out, ocean_in, ocean_sent, ocean_came)
    to_tile = (steps(block_device), cell_out, cell_in, cell_sent, cell_came)
    ocean = mask_v[...].astype(F32)
    ahead = jnp.concatenate([ocean, ocean * anomaly_v[...]], axis=0).astype(BF16)

    w2_tail = jnp.concatenate([w23_v[256:288, :]] * 4, axis=0)
    late = x + y + z >= EARLY
    first = 0
    for count in DIRECT:
        field = dot_nt(pick(first, count), adv_v[...]).astype(BF16)
        half = 0.5 * dot(field, w1_v[...])
        hidden = (half + half * jnp.tanh(half)).astype(BF16)
        main, tail = dot_nt(hidden, w23_v[0:256, :]), dot_nt(hidden, w2_tail)
        lay_out(first, count, main, tail)

        @pl.when(late)
        def _():
            if first == 0:
                pl.semaphore_wait(barrier, DEVICES - 1)
                pass_on(to_block, 0, ahead)
            issue(first, count)

        first += count

    unit = one_hot(iota((256, 256), 0) == iota((256, 256), 1))
    for b in range(HID // 256):
        rows = slice(b * 256, (b + 1) * 256)
        w1t_v[rows, :] = dot_nt(unit, w1_v[:, rows]).astype(BF16)

    w3t = w3t_v[...].astype(F32)
    w23_v[WIDTH : WIDTH + 16, :] = jnp.concatenate([w3t, jnp.zeros((12, HID), F32)], axis=0).astype(BF16)
    for c in range(COLS // WIDE):
        for b in range(HID // 256):
            first_layer(c, b)
        if c > 0:
            second_layer(c - 1)
    second_layer(COLS // WIDE - 1)

    remap = remap_v[...]
    cell = dot_nt(q_v[...], remap, lax.Precision.HIGHEST)

    @pl.when(jnp.logical_not(late))
    def _():
        pl.semaphore_wait(barrier, DEVICES - 1)
        pass_on(to_block, 0, ahead)
        issue(0, sum(DIRECT))

    pass_on(to_tile, 0, cell)

    for n, count in enumerate(CHUNKS):
        placed = dot_nt(pick(first, count), tend_v[...])
        lay_out(first, count, placed[:, 0:256], placed[:, 256:384])
        issue(first, count)
        first += count
        if n < 2:
            pass_on(to_block, n + 1, take(to_block, n).astype(BF16))
        if n > 0:
            pass_on(to_tile, n, take(to_tile, n - 1))

    slot, row = iota((256, 64), 0), iota((256, 64), 1)
    spread = one_hot((row >> 2 == slot >> 4) & ((row & 3) == (slot & 3)))
    held = (iota((256, 128), 0) & 15) >> 2 == iota((256, 128), 1) >> 5
    fold = one_hot(iota((32, 128), 0) == (iota((32, 128), 1) & 31))
    for quarter, planes in enumerate(QUARTERS):
        groups = [cores[a] * 4 + lax.rem(x - b + 4, 4) for a, b in planes]
        for group in groups:
            got = recv_v.at[pl.ds(pl.multiple_of(group * 16, 16), 16)]
            pltpu.make_async_copy(got, got, recv_sem.at[group]).wait()
        for group in groups:
            sixteen = pl.ds(pl.multiple_of(group * 16, 16), 16)
            lanes = pl.ds(pl.multiple_of(group * 256, 256), 256)
            main = jnp.concatenate([recv_v[sixteen, h : h + 4].reshape(256, 128) for h in (0, 4)], axis=1)
            layout_out[0:256, lanes] = dot_nt(unit, main).astype(BF16)
            wide = jnp.where(held, dot(spread, recv_v[sixteen, 8].reshape(64, 128)), 0.0).astype(BF16)
            layout_out[256:288, lanes] = dot_nt(fold, wide).astype(BF16)
        if quarter == 1:
            ahead = take(to_block, 2)
            masked = ahead[8:16] + ahead[0:8] * cell
            atmos_out[...] = jnp.dot(masked, remap, precision=lax.Precision.HIGHEST, preferred_element_type=F32)
        if quarter == 2:
            updated_out[...] = anomaly_v[...] + ocean * take(to_tile, 2)

    sent = send_v.at[pl.ds(0, DEVICES - 1)]
    pltpu.make_async_copy(sent, sent, send_sem).wait()
    for moves, _, in_v, gone, _ in (to_block, to_tile):
        for n, (size, _, _, _) in enumerate(moves):
            sent = in_v.at[pl.ds(4 * n, size - 1)]
            pltpu.make_async_copy(sent, sent, gone.at[n]).wait()


def hand_out(a, b, c, d, a_out, b_out, c_out, d_out, sem):
    pieces = [(b.at[rows], b_out.at[rows]) for rows in (pl.ds(k * 72, 72) for k in range(4))]
    pieces += [(a.at[rows], a_out.at[rows]) for rows in (pl.ds(k * 144, 144) for k in range(2))]
    pieces += [(c, c_out), (d, d_out)]
    copies = [pltpu.make_async_copy(source, result, sem.at[i]) for i, (source, result) in enumerate(pieces)]
    for copy in copies:
        copy.start()
    for copy in copies:
        copy.wait()


def per_device(
    atmosphere_state,
    metric,
    column_group_target,
    physics_input_layer,
    physics_tendency_layer,
    physics_flux_layer,
    block_to_tile,
    remap_weight_matrix,
    ocean_land_mask,
    ocean_sea_anomaly,
    flux_sea_response,
):
    anywhere, vmem, hbm = (pl.BlockSpec(memory_space=space) for space in (pl.ANY, pltpu.VMEM, pltpu.HBM))
    results = [
        jax.ShapeDtypeStruct((WIDTH, COLS), BF16),
        jax.ShapeDtypeStruct((WIDTH, DEVICES * CAP), BF16),
        jax.ShapeDtypeStruct((8, 128), F32),
        jax.ShapeDtypeStruct((8, 128), F32),
    ]
    done = pl.pallas_call(
        kernel,
        out_shape=results,
        in_specs=[hbm] * 12,
        out_specs=[vmem] * 4,
        scratch_shapes=[
            pltpu.VMEM((8, 128), I32),
            pltpu.VMEM((DEVICES, 384), F32),
            pltpu.VMEM((WIDTH, HID), BF16),
            pltpu.VMEM((WIDTH, COLS), BF16),
            pltpu.VMEM((2, COLS), F32),
            pltpu.VMEM((WIDTH + 16, HID), BF16),
            pltpu.VMEM((4, HID), BF16),
            pltpu.VMEM((1, 4), F32),
            pltpu.VMEM((8, 128), I32),
            pltpu.VMEM((8, 128), I32),
            pltpu.VMEM((8, 128), F32),
            pltpu.VMEM((128, 128), F32),
            pltpu.VMEM((HID, WIDTH), BF16),
            pltpu.VMEM((WIDTH, COLS), BF16),
            pltpu.VMEM((HID, COLS), BF16),
            pltpu.VMEM((384, COLS), BF16),
            pltpu.VMEM((8, 128), F32),
            pltpu.VMEM((DEVICES, ROWS, 4, 128), BF16),
            pltpu.VMEM((DEVICES, ROWS, 4, 128), BF16),
            pltpu.VMEM((3, 16, 128), BF16),
            pltpu.VMEM((16, 16, 128), BF16),
            pltpu.VMEM((3, 8, 128), F32),
            pltpu.VMEM((16, 8, 128), F32),
            pltpu.SemaphoreType.DMA((15,)),
            pltpu.SemaphoreType.DMA,
            pltpu.SemaphoreType.DMA((8,)),
            pltpu.SemaphoreType.DMA((3,)),
            pltpu.SemaphoreType.DMA((3,)),
            pltpu.SemaphoreType.DMA((3,)),
            pltpu.SemaphoreType.DMA((3,)),
        ],
        compiler_params=pltpu.CompilerParams(
            collective_id=0, has_side_effects=True, vmem_limit_bytes=VMEM_LIMIT
        ),
        name="coupling_interval",
    )(*[pltpu.with_memory_space_constraint(v, pltpu.HBM) for v in (
        column_group_target.reshape(DEVICES, 8, 128),
        jnp.asarray(tables()),
        physics_input_layer,
        atmosphere_state.reshape(WIDTH, COLS),
        metric,
        physics_tendency_layer.T,
        physics_flux_layer.T,
        flux_sea_response.reshape(1, 4),
        block_to_tile.reshape(8, 128),
        ocean_land_mask,
        ocean_sea_anomaly,
        remap_weight_matrix,
    )])
    stepped, layout, updated, atmos = pl.pallas_call(
        hand_out,
        out_shape=results,
        in_specs=[anywhere] * 4,
        out_specs=[anywhere] * 4,
        scratch_shapes=[pltpu.SemaphoreType.DMA((8,))],
        compiler_params=pltpu.CompilerParams(vmem_limit_bytes=4 * 1024 * 1024),
        name="hand_out",
    )(*done)
    return (
        stepped.reshape(atmosphere_state.shape),
        layout.T,
        updated,
        atmos.reshape(COLS),
    )


def solution(mesh):
    placed = (
        P(None, None, ("sect", "dev")),
        P(None, ("sect", "dev")),
        P(),
        P(),
        P(),
        P(),
        P(),
        P(),
        P(("sect", "dev"), None),
        P(("sect", "dev"), None),
        P(),
    )
    return jax.shard_map(
        per_device,
        mesh=mesh,
        in_specs=placed,
        out_specs=(
            P(None, None, ("sect", "dev")),
            P(("sect", "dev"), None),
            P(("sect", "dev"), None),
            P(("sect", "dev")),
        ),
        check_vma=False,
    )
```

```python
import functools
import itertools
import random

import jax
import jax.numpy as jnp
import numpy as np
from jax import lax
from jax.experimental import pallas as pl
from jax.experimental.pallas import tpu as pltpu
from jax.sharding import PartitionSpec as P

MESH = pl.DeviceIdType.MESH
BF16 = jnp.bfloat16
F32 = jnp.float32
I32 = jnp.int32

DEVICES = 128
CAP = 16
COLS = 1024
WIDTH = 288
HID = 1024
ROWS = 9
STEP = 256
WIDE = 512
EARLY = 5
VMEM_LIMIT = 32 * 1024 * 1024
NT = (((1,), (1,)), ((), ()))


def gll_tables():
    gll_nodes = np.array([-1.0, -1.0 / np.sqrt(5.0), 1.0 / np.sqrt(5.0), 1.0])
    offdiag = gll_nodes[:, None] - gll_nodes[None, :] + np.eye(4)
    bary = np.prod(offdiag, axis=1)
    derivative = bary[:, None] / (bary[None, :] * offdiag)
    diag_sum = np.sum(1.0 / offdiag - np.eye(4), axis=1)
    derivative = derivative * (1.0 - np.eye(4)) + np.eye(4) * diag_sum[:, None]
    first_dir = np.kron(np.eye(8), np.kron(np.eye(4), derivative)).T
    second_dir = np.kron(np.eye(8), np.kron(derivative, np.eye(4))).T
    return np.concatenate([first_dir, second_dir], axis=1)


QUARTERS = [[(0, 1), (0, 3)], [(1, 1), (1, 3)], [(0, 2), (1, 2), (1, 0)], [(0, 0)]]


def message_order():
    hops = lambda k: min(k, 4 - k)
    mixed, order = random.Random(1), []
    for planes in QUARTERS:
        part = [plane + yz for plane in planes for yz in itertools.product(range(4), range(4))]
        mixed.shuffle(part)
        part.sort(key=lambda o: (o == SELF, -sum(hops(k) for k in o[1:])))
        order += part
    return order


SELF = (0, 0, 0, 0)
ORDER = message_order()
FAR_FIRST = sorted(ORDER, key=lambda o: -sum(min(k, 4 - k) for k in o[1:]))
DIRECT = [16, 16]
CHUNKS = [32, 32, 32]


def tables():
    table = np.zeros((DEVICES, 384), np.float32)
    table[:, :256] = gll_tables()
    table[:, 256:260] = ORDER
    return table


def device(index):
    return (lax.div(index, 64), lax.rem(index, 64))


def dot(a, b):
    return jnp.dot(a, b, preferred_element_type=F32)


def dot_nt(a, b, precision=None):
    return lax.dot_general(a, b, NT, precision=precision, preferred_element_type=F32)


def iota(shape, dim):
    return lax.broadcasted_iota(I32, shape, dim)


def one_hot(condition):
    return jnp.where(condition, 1.0, 0.0).astype(BF16)


def kernel(
    target_hbm,
    table_hbm,
    w1_hbm,
    state_hbm,
    metric_hbm,
    w2t_hbm,
    w3t_hbm,
    response_hbm,
    tile_hbm,
    mask_hbm,
    anomaly_hbm,
    remap_hbm,
    stepped_out,
    layout_out,
    updated_out,
    atmos_out,
    target_v,
    table_v,
    w1_v,
    x_v,
    metric_v,
    w23_v,
    w3t_v,
    response_v,
    tile_v,
    mask_v,
    anomaly_v,
    remap_v,
    w1t_v,
    adv_v,
    hid_v,
    tend_v,
    q_v,
    send_v,
    recv_v,
    ocean_out,
    ocean_in,
    cell_out,
    cell_in,
    in_sem,
    send_sem,
    recv_sem,
    ocean_sent,
    ocean_came,
    cell_sent,
    cell_came,
):
    core, chip = lax.axis_index("sect"), lax.axis_index("dev")
    me = core * 64 + chip
    x, y, z = lax.div(chip, 16), lax.rem(lax.div(chip, 4), 4), lax.rem(chip, 4)

    half = COLS // 2
    pairs = [
        (target_hbm.at[me], target_v),
        (table_hbm, table_v),
        (metric_hbm, metric_v),
        (state_hbm.at[:, pl.ds(0, half)], x_v.at[:, pl.ds(0, half)]),
        (state_hbm.at[:, pl.ds(half, half)], x_v.at[:, pl.ds(half, half)]),
        (w1_hbm.at[:, pl.ds(0, half)], w1_v.at[:, pl.ds(0, half)]),
        (w1_hbm.at[:, pl.ds(half, half)], w1_v.at[:, pl.ds(half, half)]),
        (w2t_hbm.at[:, pl.ds(0, half)], w23_v.at[pl.ds(0, WIDTH), pl.ds(0, half)]),
        (w2t_hbm.at[:, pl.ds(half, half)], w23_v.at[pl.ds(0, WIDTH), pl.ds(half, half)]),
        (w3t_hbm, w3t_v),
        (response_hbm, response_v),
        (tile_hbm, tile_v),
        (mask_hbm, mask_v),
        (anomaly_hbm, anomaly_v),
        (remap_hbm, remap_v),
    ]
    loads = [pltpu.make_async_copy(a, b, in_sem.at[i]) for i, (a, b) in enumerate(pairs)]
    for load in loads:
        load.start()

    cores = [lax.rem(core + k, 2) for k in range(2)]
    xs = [lax.rem(x + k, 4) * 16 for k in range(4)]
    ys = [lax.rem(y + k, 4) * 4 for k in range(4)]
    zs = [lax.rem(z + k, 4) for k in range(4)]
    barrier = pltpu.get_barrier_semaphore()
    for a, b, e, f in FAR_FIRST:
        if (a, b, e, f) != SELF:
            pl.semaphore_signal(barrier, inc=1, device_id=(cores[a], xs[b] + ys[e] + zs[f]), device_id_type=MESH)

    for load in loads[0:5]:
        load.wait()
    deriv = table_v[:, 0:256].astype(BF16)

    def dynamics(b):
        at = slice(b * 128, (b + 1) * 128)
        field = x_v[:, at]
        grads = dot(field, deriv)
        wide = field.astype(F32)
        wind_first = wide[0:72] * metric_v[0:1, at]
        wind_second = wide[72:144] * metric_v[1:2, at]
        moved = (
            wide
            - jnp.concatenate([wind_first] * 4, axis=0) * grads[:, 0:128]
            - jnp.concatenate([wind_second] * 4, axis=0) * grads[:, 128:256]
        )
        adv_v[:, at] = moved.astype(BF16)

    def first_layer(c, b):
        at, rows = slice(c * WIDE, (c + 1) * WIDE), slice(b * 256, (b + 1) * 256)
        half = 0.5 * dot(w1t_v[rows, :], adv_v[:, at])
        hid_v[rows, at] = (half + half * jnp.tanh(half)).astype(BF16)

    def second_layer(c):
        at = slice(c * WIDE, (c + 1) * WIDE)
        result = dot(w23_v[...], hid_v[:, at])
        tendency = result[0:WIDTH]
        stepped_out[:, at] = (adv_v[:, at].astype(F32) + tendency).astype(BF16)
        tendency = tendency.astype(BF16)
        tend_v[0:WIDTH, at] = tendency
        for g in range(1, 4):
            tend_v[256 + 32 * g : 288 + 32 * g, at] = tendency[256:288]
        flux = result[WIDTH : WIDTH + 8].astype(BF16).astype(F32)
        mixed = sum(response_v[:, k : k + 1] * flux[k : k + 1] for k in range(4))
        for b in range(WIDE // 128):
            j = c * (WIDE // 128) + b
            q_v[j : j + 1, :] = mixed[:, b * 128 : (b + 1) * 128]

    for b in range(COLS // 128):
        dynamics(b)

    order = table_v[:, 256:384].astype(I32)
    to_device = (
        ((order[:, 0:1] + core) & 1) * 64
        + ((order[:, 1:2] + x) & 3) * 16
        + ((order[:, 2:3] + y) & 3) * 4
        + ((order[:, 3:4] + z) & 3)
    )

    targets = jnp.concatenate([target_v[k : k + 1, :] for k in range(8)], axis=1)
    before = one_hot(iota((STEP, STEP), 0) < iota((STEP, STEP), 1))
    message = iota((DEVICES, STEP), 0)
    taken = jnp.zeros((DEVICES, 1), F32)
    slots = []
    for c in range(COLS // STEP):
        hit = to_device == targets[:, c * STEP : (c + 1) * STEP]
        hits = jnp.where(hit, 1.0, 0.0)
        earlier = dot(hits.astype(BF16), before) + taken
        taken = taken + jnp.sum(hits, axis=1, keepdims=True)
        slot = jnp.where(hit, earlier.astype(I32) + CAP * message, 0)
        slots.append(jnp.sum(slot, axis=0, keepdims=True))
    slots = jnp.concatenate(slots, axis=1)

    plane = lax.div(me, 16)

    def lay_out(first, count, main, tail):
        size, into = count * CAP, pl.ds(first, count)
        main = main.astype(BF16)
        send_v[into, 0:4] = main[:, 0:128].reshape(count, 4, 4, 128)
        send_v[into, 4:8] = main[:, 128:256].reshape(count, 4, 4, 128)
        keep = (iota((size, 128), 0) & 15) >> 2 == iota((size, 128), 1) >> 5
        tail = jnp.where(keep, tail, 0.0).reshape(count, CAP, 128)
        tail = tail[:, 0:8] + tail[:, 8:16]
        send_v[into, 8] = (tail[:, 0:4] + tail[:, 4:8]).astype(BF16)

    def issue(first, count):
        for i in range(first, first + count):
            a, b, e, f = ORDER[i]
            if ORDER[i] == SELF:
                pltpu.make_async_copy(send_v.at[i], recv_v.at[me], recv_sem.at[plane]).start()
                continue
            pltpu.make_async_remote_copy(
                send_v.at[i],
                recv_v.at[me],
                send_sem,
                recv_sem.at[plane],
                device_id=(cores[a], xs[b] + ys[e] + zs[f]),
                device_id_type=MESH,
            ).start()

    def pick(first, count):
        return one_hot(iota((count * CAP, COLS), 0) + first * CAP == slots)

    for load in loads[5:]:
        load.wait()
    lane, sub = iota((8, 128), 1), iota((8, 128), 0)
    shift_row = jnp.where(iota((1, 128), 1) < 8, tile_v[0:1, :] >> 3, -1)
    shift_col = jnp.sum(jnp.where(lane == sub, shift_row, 0), axis=1, keepdims=True)

    def steps(devices):
        return [
            (4, z, devices & 3, lambda k: plane * 16 + y * 4 + k),
            (4, y, (devices >> 2) & 3, lambda k: plane * 16 + k * 4 + z),
            (8, plane, devices >> 4, lambda k: k * 16 + y * 4 + z),
        ]

    def pass_on(way, n, rows):
        (moves, out_v, in_v, sent, came) = way
        size, mine, _, peer = moves[n]
        out_v[n] = rows
        in_v[4 * n + mine] = rows
        for k in range(1, size):
            pltpu.make_async_remote_copy(
                out_v.at[n],
                in_v.at[4 * n + mine],
                sent.at[n],
                came.at[n],
                device_id=device(peer(lax.rem(mine + k, size))),
                device_id_type=MESH,
            ).start()

    def take(way, n):
        (moves, _, in_v, _, came) = way
        size, _, source, _ = moves[n]
        got = in_v.at[pl.ds(4 * n, size - 1)]
        pltpu.make_async_copy(got, got, came.at[n]).wait()
        chosen = jnp.zeros(in_v.shape[1:], F32)
        for k in range(size):
            chosen = chosen + jnp.where(source == k, in_v[4 * n + k].astype(F32), 0.0)
        return chosen

    tile_device = (me + jnp.concatenate([shift_col, shift_col], axis=0)) & (DEVICES - 1)
    block_device = (me - shift_col) & (DEVICES - 1)
    to_block = (steps(tile_device), ocean_out, ocean_in, ocean_sent, ocean_came)
    to_tile = (steps(block_device), cell_out, cell_in, cell_sent, cell_came)
    ocean = mask_v[...].astype(F32)
    ahead = jnp.concatenate([ocean, ocean * anomaly_v[...]], axis=0).astype(BF16)

    w2_tail = jnp.concatenate([w23_v[256:288, :]] * 4, axis=0)
    late = x + y + z >= EARLY
    first = 0
    for count in DIRECT:
        field = dot_nt(pick(first, count), adv_v[...]).astype(BF16)
        half = 0.5 * dot(field, w1_v[...])
        hidden = (half + half * jnp.tanh(half)).astype(BF16)
        main, tail = dot_nt(hidden, w23_v[0:256, :]), dot_nt(hidden, w2_tail)
        lay_out(first, count, main, tail)

        @pl.when(late)
        def _():
            if first == 0:
                pl.semaphore_wait(barrier, DEVICES - 1)
                pass_on(to_block, 0, ahead)
            issue(first, count)

        first += count

    unit = one_hot(iota((256, 256), 0) == iota((256, 256), 1))
    for b in range(HID // 256):
        rows = slice(b * 256, (b + 1) * 256)
        w1t_v[rows, :] = dot_nt(unit, w1_v[:, rows]).astype(BF16)

    w3t = w3t_v[...].astype(F32)
    w23_v[WIDTH : WIDTH + 16, :] = jnp.concatenate([w3t, jnp.zeros((12, HID), F32)], axis=0).astype(BF16)
    for c in range(COLS // WIDE):
        for b in range(HID // 256):
            first_layer(c, b)
        if c > 0:
            second_layer(c - 1)
    second_layer(COLS // WIDE - 1)

    remap = remap_v[...]
    cell = dot_nt(q_v[...], remap, lax.Precision.HIGHEST)

    @pl.when(jnp.logical_not(late))
    def _():
        pl.semaphore_wait(barrier, DEVICES - 1)
        pass_on(to_block, 0, ahead)
        issue(0, sum(DIRECT))

    pass_on(to_tile, 0, cell)

    for n, count in enumerate(CHUNKS):
        placed = dot_nt(pick(first, count), tend_v[...])
        lay_out(first, count, placed[:, 0:256], placed[:, 256:384])
        issue(first, count)
        first += count
        if n < 2:
            pass_on(to_block, n + 1, take(to_block, n).astype(BF16))
        if n > 0:
            pass_on(to_tile, n, take(to_tile, n - 1))

    slot, row = iota((256, 64), 0), iota((256, 64), 1)
    spread = one_hot((row >> 2 == slot >> 4) & ((row & 3) == (slot & 3)))
    held = (iota((256, 128), 0) & 15) >> 2 == iota((256, 128), 1) >> 5
    fold = one_hot(iota((32, 128), 0) == (iota((32, 128), 1) & 31))
    for quarter, planes in enumerate(QUARTERS):
        groups = [cores[a] * 4 + lax.rem(x - b + 4, 4) for a, b in planes]
        for group in groups:
            got = recv_v.at[pl.ds(pl.multiple_of(group * 16, 16), 16)]
            pltpu.make_async_copy(got, got, recv_sem.at[group]).wait()
        for group in groups:
            sixteen = pl.ds(pl.multiple_of(group * 16, 16), 16)
            lanes = pl.ds(pl.multiple_of(group * 256, 256), 256)
            main = jnp.concatenate([recv_v[sixteen, h : h + 4].reshape(256, 128) for h in (0, 4)], axis=1)
            layout_out[0:256, lanes] = dot_nt(unit, main).astype(BF16)
            wide = jnp.where(held, dot(spread, recv_v[sixteen, 8].reshape(64, 128)), 0.0).astype(BF16)
            layout_out[256:288, lanes] = dot_nt(fold, wide).astype(BF16)
        if quarter == 1:
            ahead = take(to_block, 2)
            masked = ahead[8:16] + ahead[0:8] * cell
            atmos_out[...] = jnp.dot(masked, remap, precision=lax.Precision.HIGHEST, preferred_element_type=F32)
        if quarter == 2:
            updated_out[...] = anomaly_v[...] + ocean * take(to_tile, 2)

    sent = send_v.at[pl.ds(0, DEVICES - 1)]
    pltpu.make_async_copy(sent, sent, send_sem).wait()
    for moves, _, in_v, gone, _ in (to_block, to_tile):
        for n, (size, _, _, _) in enumerate(moves):
            sent = in_v.at[pl.ds(4 * n, size - 1)]
            pltpu.make_async_copy(sent, sent, gone.at[n]).wait()


def hand_out(a, b, c, d, a_out, b_out, c_out, d_out, sem):
    pieces = [(b.at[rows], b_out.at[rows]) for rows in (pl.ds(k * 72, 72) for k in range(4))]
    pieces += [(a.at[rows], a_out.at[rows]) for rows in (pl.ds(k * 144, 144) for k in range(2))]
    pieces += [(c, c_out), (d, d_out)]
    copies = [pltpu.make_async_copy(source, result, sem.at[i]) for i, (source, result) in enumerate(pieces)]
    for copy in copies:
        copy.start()
    for copy in copies:
        copy.wait()


def per_device(
    atmosphere_state,
    metric,
    column_group_target,
    physics_input_layer,
    physics_tendency_layer,
    physics_flux_layer,
    block_to_tile,
    remap_weight_matrix,
    ocean_land_mask,
    ocean_sea_anomaly,
    flux_sea_response,
):
    anywhere, vmem, hbm = (pl.BlockSpec(memory_space=space) for space in (pl.ANY, pltpu.VMEM, pltpu.HBM))
    results = [
        jax.ShapeDtypeStruct((WIDTH, COLS), BF16),
        jax.ShapeDtypeStruct((WIDTH, DEVICES * CAP), BF16),
        jax.ShapeDtypeStruct((8, 128), F32),
        jax.ShapeDtypeStruct((8, 128), F32),
    ]
    done = pl.pallas_call(
        kernel,
        out_shape=results,
        in_specs=[hbm] * 12,
        out_specs=[vmem] * 4,
        scratch_shapes=[
            pltpu.VMEM((8, 128), I32),
            pltpu.VMEM((DEVICES, 384), F32),
            pltpu.VMEM((WIDTH, HID), BF16),
            pltpu.VMEM((WIDTH, COLS), BF16),
            pltpu.VMEM((2, COLS), F32),
            pltpu.VMEM((WIDTH + 16, HID), BF16),
            pltpu.VMEM((4, HID), BF16),
            pltpu.VMEM((1, 4), F32),
            pltpu.VMEM((8, 128), I32),
            pltpu.VMEM((8, 128), I32),
            pltpu.VMEM((8, 128), F32),
            pltpu.VMEM((128, 128), F32),
            pltpu.VMEM((HID, WIDTH), BF16),
            pltpu.VMEM((WIDTH, COLS), BF16),
            pltpu.VMEM((HID, COLS), BF16),
            pltpu.VMEM((384, COLS), BF16),
            pltpu.VMEM((8, 128), F32),
            pltpu.VMEM((DEVICES, ROWS, 4, 128), BF16),
            pltpu.VMEM((DEVICES, ROWS, 4, 128), BF16),
            pltpu.VMEM((3, 16, 128), BF16),
            pltpu.VMEM((16, 16, 128), BF16),
            pltpu.VMEM((3, 8, 128), F32),
            pltpu.VMEM((16, 8, 128), F32),
            pltpu.SemaphoreType.DMA((15,)),
            pltpu.SemaphoreType.DMA,
            pltpu.SemaphoreType.DMA((8,)),
            pltpu.SemaphoreType.DMA((3,)),
            pltpu.SemaphoreType.DMA((3,)),
            pltpu.SemaphoreType.DMA((3,)),
            pltpu.SemaphoreType.DMA((3,)),
        ],
        compiler_params=pltpu.CompilerParams(
            collective_id=0, has_side_effects=True, vmem_limit_bytes=VMEM_LIMIT
        ),
        name="coupling_interval",
    )(*[pltpu.with_memory_space_constraint(v, pltpu.HBM) for v in (
        column_group_target.reshape(DEVICES, 8, 128),
        jnp.asarray(tables()),
        physics_input_layer,
        atmosphere_state.reshape(WIDTH, COLS),
        metric,
        physics_tendency_layer.T,
        physics_flux_layer.T,
        flux_sea_response.reshape(1, 4),
        block_to_tile.reshape(8, 128),
        ocean_land_mask,
        ocean_sea_anomaly,
        remap_weight_matrix,
    )])
    stepped, layout, updated, atmos = pl.pallas_call(
        hand_out,
        out_shape=results,
        in_specs=[anywhere] * 4,
        out_specs=[anywhere] * 4,
        scratch_shapes=[pltpu.SemaphoreType.DMA((8,))],
        compiler_params=pltpu.CompilerParams(vmem_limit_bytes=4 * 1024 * 1024),
        name="hand_out",
    )(*done)
    return (
        stepped.reshape(atmosphere_state.shape),
        layout.T,
        updated,
        atmos.reshape(COLS),
    )


def solution(mesh):
    placed = (
        P(None, None, ("sect", "dev")),
        P(None, ("sect", "dev")),
        P(),
        P(),
        P(),
        P(),
        P(),
        P(),
        P(("sect", "dev"), None),
        P(("sect", "dev"), None),
        P(),
    )
    return jax.shard_map(
        per_device,
        mesh=mesh,
        in_specs=placed,
        out_specs=(
            P(None, None, ("sect", "dev")),
            P(("sect", "dev"), None),
            P(("sect", "dev"), None),
            P(("sect", "dev")),
        ),
        check_vma=False,
    )
```

```python
import functools
import itertools
import random

import jax
import jax.numpy as jnp
import numpy as np
from jax import lax
from jax.experimental import pallas as pl
from jax.experimental.pallas import tpu as pltpu
from jax.sharding import PartitionSpec as P

MESH = pl.DeviceIdType.MESH
BF16 = jnp.bfloat16
F32 = jnp.float32
I32 = jnp.int32

DEVICES = 128
CAP = 16
COLS = 1024
WIDTH = 288
HID = 1024
ROWS = 9
STEP = 256
WIDE = 512
EARLY = 5
VMEM_LIMIT = 32 * 1024 * 1024
NT = (((1,), (1,)), ((), ()))


def gll_tables():
    gll_nodes = np.array([-1.0, -1.0 / np.sqrt(5.0), 1.0 / np.sqrt(5.0), 1.0])
    offdiag = gll_nodes[:, None] - gll_nodes[None, :] + np.eye(4)
    bary = np.prod(offdiag, axis=1)
    derivative = bary[:, None] / (bary[None, :] * offdiag)
    diag_sum = np.sum(1.0 / offdiag - np.eye(4), axis=1)
    derivative = derivative * (1.0 - np.eye(4)) + np.eye(4) * diag_sum[:, None]
    first_dir = np.kron(np.eye(8), np.kron(np.eye(4), derivative)).T
    second_dir = np.kron(np.eye(8), np.kron(derivative, np.eye(4))).T
    return np.concatenate([first_dir, second_dir], axis=1)


QUARTERS = [[(0, 1), (0, 3)], [(1, 1), (1, 3)], [(0, 2), (1, 2), (1, 0)], [(0, 0)]]


def message_order():
    hops = lambda k: min(k, 4 - k)
    mixed, order = random.Random(1), []
    for planes in QUARTERS:
        part = [plane + yz for plane in planes for yz in itertools.product(range(4), range(4))]
        mixed.shuffle(part)
        part.sort(key=lambda o: (o == SELF, -sum(hops(k) for k in o[1:])))
        order += part
    return order


SELF = (0, 0, 0, 0)
ORDER = message_order()
FAR_FIRST = sorted(ORDER, key=lambda o: -sum(min(k, 4 - k) for k in o[1:]))
DIRECT = [16, 16]
CHUNKS = [32, 32, 32]


def tables():
    table = np.zeros((DEVICES, 384), np.float32)
    table[:, :256] = gll_tables()
    table[:, 256:260] = ORDER
    return table


def device(index):
    return (lax.div(index, 64), lax.rem(index, 64))


def dot(a, b):
    return jnp.dot(a, b, preferred_element_type=F32)


def dot_nt(a, b, precision=None):
    return lax.dot_general(a, b, NT, precision=precision, preferred_element_type=F32)


def iota(shape, dim):
    return lax.broadcasted_iota(I32, shape, dim)


def one_hot(condition):
    return jnp.where(condition, 1.0, 0.0).astype(BF16)


def unpack(messages, lanes_out):
    unit = one_hot(iota((256, 256), 0) == iota((256, 256), 1))
    slot, row = iota((256, 64), 0), iota((256, 64), 1)
    spread = one_hot((row >> 2 == slot >> 4) & ((row & 3) == (slot & 3)))
    held = (iota((256, 128), 0) & 15) >> 2 == iota((256, 128), 1) >> 5
    fold = one_hot(iota((32, 128), 0) == (iota((32, 128), 1) & 31))
    main = jnp.concatenate([messages[:, h : h + 4].reshape(256, 128) for h in (0, 4)], axis=1)
    lanes_out[0:256, :] = dot_nt(unit, main).astype(BF16)
    wide = jnp.where(held, dot(spread, messages[:, 8].reshape(64, 128)), 0.0).astype(BF16)
    lanes_out[256:288, :] = dot_nt(fold, wide).astype(BF16)


def kernel(
    target_hbm,
    table_hbm,
    w1_hbm,
    state_hbm,
    metric_hbm,
    w2t_hbm,
    w3t_hbm,
    response_hbm,
    tile_hbm,
    mask_hbm,
    anomaly_hbm,
    remap_hbm,
    stepped_out,
    layout_out,
    updated_out,
    atmos_out,
    own_out,
    target_v,
    table_v,
    w1_v,
    x_v,
    metric_v,
    w23_v,
    w3t_v,
    response_v,
    tile_v,
    mask_v,
    anomaly_v,
    remap_v,
    w1t_v,
    adv_v,
    hid_v,
    tend_v,
    q_v,
    send_v,
    recv_v,
    ocean_out,
    ocean_in,
    cell_out,
    cell_in,
    in_sem,
    send_sem,
    recv_sem,
    ocean_sent,
    ocean_came,
    cell_sent,
    cell_came,
):
    core, chip = lax.axis_index("sect"), lax.axis_index("dev")
    me = core * 64 + chip
    x, y, z = lax.div(chip, 16), lax.rem(lax.div(chip, 4), 4), lax.rem(chip, 4)

    half = COLS // 2
    pairs = [
        (target_hbm.at[me], target_v),
        (table_hbm, table_v),
        (metric_hbm, metric_v),
        (state_hbm.at[:, pl.ds(0, half)], x_v.at[:, pl.ds(0, half)]),
        (state_hbm.at[:, pl.ds(half, half)], x_v.at[:, pl.ds(half, half)]),
        (w1_hbm.at[:, pl.ds(0, half)], w1_v.at[:, pl.ds(0, half)]),
        (w1_hbm.at[:, pl.ds(half, half)], w1_v.at[:, pl.ds(half, half)]),
        (w2t_hbm.at[:, pl.ds(0, half)], w23_v.at[pl.ds(0, WIDTH), pl.ds(0, half)]),
        (w2t_hbm.at[:, pl.ds(half, half)], w23_v.at[pl.ds(0, WIDTH), pl.ds(half, half)]),
        (w3t_hbm, w3t_v),
        (response_hbm, response_v),
        (tile_hbm, tile_v),
        (mask_hbm, mask_v),
        (anomaly_hbm, anomaly_v),
        (remap_hbm, remap_v),
    ]
    loads = [pltpu.make_async_copy(a, b, in_sem.at[i]) for i, (a, b) in enumerate(pairs)]
    for load in loads:
        load.start()

    cores = [lax.rem(core + k, 2) for k in range(2)]
    xs = [lax.rem(x + k, 4) * 16 for k in range(4)]
    ys = [lax.rem(y + k, 4) * 4 for k in range(4)]
    zs = [lax.rem(z + k, 4) for k in range(4)]
    barrier = pltpu.get_barrier_semaphore()
    for a, b, e, f in FAR_FIRST:
        if (a, b, e, f) != SELF:
            pl.semaphore_signal(barrier, inc=1, device_id=(cores[a], xs[b] + ys[e] + zs[f]), device_id_type=MESH)

    for load in loads[0:5]:
        load.wait()
    deriv = table_v[:, 0:256].astype(BF16)

    def dynamics(b):
        at = slice(b * 128, (b + 1) * 128)
        field = x_v[:, at]
        grads = dot(field, deriv)
        wide = field.astype(F32)
        wind_first = wide[0:72] * metric_v[0:1, at]
        wind_second = wide[72:144] * metric_v[1:2, at]
        moved = (
            wide
            - jnp.concatenate([wind_first] * 4, axis=0) * grads[:, 0:128]
            - jnp.concatenate([wind_second] * 4, axis=0) * grads[:, 128:256]
        )
        adv_v[:, at] = moved.astype(BF16)

    def first_layer(c, b):
        at, rows = slice(c * WIDE, (c + 1) * WIDE), slice(b * 256, (b + 1) * 256)
        half = 0.5 * dot(w1t_v[rows, :], adv_v[:, at])
        hid_v[rows, at] = (half + half * jnp.tanh(half)).astype(BF16)

    def second_layer(c):
        at = slice(c * WIDE, (c + 1) * WIDE)
        result = dot(w23_v[...], hid_v[:, at])
        tendency = result[0:WIDTH]
        stepped_out[:, at] = (adv_v[:, at].astype(F32) + tendency).astype(BF16)
        tendency = tendency.astype(BF16)
        tend_v[0:WIDTH, at] = tendency
        for g in range(1, 4):
            tend_v[256 + 32 * g : 288 + 32 * g, at] = tendency[256:288]
        flux = result[WIDTH : WIDTH + 8].astype(BF16).astype(F32)
        mixed = sum(response_v[:, k : k + 1] * flux[k : k + 1] for k in range(4))
        for b in range(WIDE // 128):
            j = c * (WIDE // 128) + b
            q_v[j : j + 1, :] = mixed[:, b * 128 : (b + 1) * 128]

    for b in range(COLS // 128):
        dynamics(b)

    order = table_v[:, 256:384].astype(I32)
    to_device = (
        ((order[:, 0:1] + core) & 1) * 64
        + ((order[:, 1:2] + x) & 3) * 16
        + ((order[:, 2:3] + y) & 3) * 4
        + ((order[:, 3:4] + z) & 3)
    )

    targets = jnp.concatenate([target_v[k : k + 1, :] for k in range(8)], axis=1)
    before = one_hot(iota((STEP, STEP), 0) < iota((STEP, STEP), 1))
    message = iota((DEVICES, STEP), 0)
    taken = jnp.zeros((DEVICES, 1), F32)
    slots = []
    for c in range(COLS // STEP):
        hit = to_device == targets[:, c * STEP : (c + 1) * STEP]
        hits = jnp.where(hit, 1.0, 0.0)
        earlier = dot(hits.astype(BF16), before) + taken
        taken = taken + jnp.sum(hits, axis=1, keepdims=True)
        slot = jnp.where(hit, earlier.astype(I32) + CAP * message, 0)
        slots.append(jnp.sum(slot, axis=0, keepdims=True))
    slots = jnp.concatenate(slots, axis=1)

    plane = lax.div(me, 16)

    def lay_out(first, count, main, tail):
        size, into = count * CAP, pl.ds(first, count)
        main = main.astype(BF16)
        send_v[into, 0:4] = main[:, 0:128].reshape(count, 4, 4, 128)
        send_v[into, 4:8] = main[:, 128:256].reshape(count, 4, 4, 128)
        keep = (iota((size, 128), 0) & 15) >> 2 == iota((size, 128), 1) >> 5
        tail = jnp.where(keep, tail, 0.0).reshape(count, CAP, 128)
        tail = tail[:, 0:8] + tail[:, 8:16]
        send_v[into, 8] = (tail[:, 0:4] + tail[:, 4:8]).astype(BF16)

    def issue(first, count):
        for i in range(first, first + count):
            a, b, e, f = ORDER[i]
            if ORDER[i] == SELF:
                pltpu.make_async_copy(send_v.at[i], recv_v.at[me], recv_sem.at[plane]).start()
                continue
            pltpu.make_async_remote_copy(
                send_v.at[i],
                recv_v.at[me],
                send_sem,
                recv_sem.at[plane],
                device_id=(cores[a], xs[b] + ys[e] + zs[f]),
                device_id_type=MESH,
            ).start()

    def pick(first, count):
        return one_hot(iota((count * CAP, COLS), 0) + first * CAP == slots)

    for load in loads[5:]:
        load.wait()
    lane, sub = iota((8, 128), 1), iota((8, 128), 0)
    shift_row = jnp.where(iota((1, 128), 1) < 8, tile_v[0:1, :] >> 3, -1)
    shift_col = jnp.sum(jnp.where(lane == sub, shift_row, 0), axis=1, keepdims=True)

    def steps(devices):
        return [
            (4, z, devices & 3, lambda k: plane * 16 + y * 4 + k),
            (4, y, (devices >> 2) & 3, lambda k: plane * 16 + k * 4 + z),
            (8, plane, devices >> 4, lambda k: k * 16 + y * 4 + z),
        ]

    def pass_on(way, n, rows):
        (moves, out_v, in_v, sent, came) = way
        size, mine, _, peer = moves[n]
        out_v[n] = rows
        in_v[4 * n + mine] = rows
        for k in range(1, size):
            pltpu.make_async_remote_copy(
                out_v.at[n],
                in_v.at[4 * n + mine],
                sent.at[n],
                came.at[n],
                device_id=device(peer(lax.rem(mine + k, size))),
                device_id_type=MESH,
            ).start()

    def take(way, n):
        (moves, _, in_v, _, came) = way
        size, _, source, _ = moves[n]
        got = in_v.at[pl.ds(4 * n, size - 1)]
        pltpu.make_async_copy(got, got, came.at[n]).wait()
        chosen = jnp.zeros(in_v.shape[1:], F32)
        for k in range(size):
            chosen = chosen + jnp.where(source == k, in_v[4 * n + k].astype(F32), 0.0)
        return chosen

    tile_device = (me + jnp.concatenate([shift_col, shift_col], axis=0)) & (DEVICES - 1)
    block_device = (me - shift_col) & (DEVICES - 1)
    to_block = (steps(tile_device), ocean_out, ocean_in, ocean_sent, ocean_came)
    to_tile = (steps(block_device), cell_out, cell_in, cell_sent, cell_came)
    ocean = mask_v[...].astype(F32)
    ahead = jnp.concatenate([ocean, ocean * anomaly_v[...]], axis=0).astype(BF16)

    w2_tail = jnp.concatenate([w23_v[256:288, :]] * 4, axis=0)
    late = x + y + z >= EARLY
    first = 0
    for count in DIRECT:
        field = dot_nt(pick(first, count), adv_v[...]).astype(BF16)
        half = 0.5 * dot(field, w1_v[...])
        hidden = (half + half * jnp.tanh(half)).astype(BF16)
        main, tail = dot_nt(hidden, w23_v[0:256, :]), dot_nt(hidden, w2_tail)
        lay_out(first, count, main, tail)

        @pl.when(late)
        def _():
            if first == 0:
                pl.semaphore_wait(barrier, DEVICES - 1)
                pass_on(to_block, 0, ahead)
            issue(first, count)

        first += count

    unit = one_hot(iota((256, 256), 0) == iota((256, 256), 1))
    for b in range(HID // 256):
        rows = slice(b * 256, (b + 1) * 256)
        w1t_v[rows, :] = dot_nt(unit, w1_v[:, rows]).astype(BF16)

    w3t = w3t_v[...].astype(F32)
    w23_v[WIDTH : WIDTH + 16, :] = jnp.concatenate([w3t, jnp.zeros((12, HID), F32)], axis=0).astype(BF16)
    for c in range(COLS // WIDE):
        for b in range(HID // 256):
            first_layer(c, b)
        if c > 0:
            second_layer(c - 1)
    second_layer(COLS // WIDE - 1)

    remap = remap_v[...]
    cell = dot_nt(q_v[...], remap, lax.Precision.HIGHEST)

    @pl.when(jnp.logical_not(late))
    def _():
        pl.semaphore_wait(barrier, DEVICES - 1)
        pass_on(to_block, 0, ahead)
        issue(0, sum(DIRECT))

    pass_on(to_tile, 0, cell)

    for n, count in enumerate(CHUNKS):
        placed = dot_nt(pick(first, count), tend_v[...])
        lay_out(first, count, placed[:, 0:256], placed[:, 256:384])
        issue(first, count)
        first += count
        if n < 2:
            pass_on(to_block, n + 1, take(to_block, n).astype(BF16))
        if n > 0:
            pass_on(to_tile, n, take(to_tile, n - 1))

    for quarter, planes in enumerate(QUARTERS):
        groups = [cores[a] * 4 + lax.rem(x - b + 4, 4) for a, b in planes]
        for group in groups:
            got = recv_v.at[pl.ds(pl.multiple_of(group * 16, 16), 16)]
            pltpu.make_async_copy(got, got, recv_sem.at[group]).wait()
        for group in groups:
            sixteen = pl.ds(pl.multiple_of(group * 16, 16), 16)
            if quarter == len(QUARTERS) - 1:
                own_out[...] = recv_v[sixteen]
                continue
            lanes = pl.ds(pl.multiple_of(group * 256, 256), 256)
            unpack(recv_v.at[sixteen], layout_out.at[:, lanes])
        if quarter == 1:
            ahead = take(to_block, 2)
            masked = ahead[8:16] + ahead[0:8] * cell
            atmos_out[...] = jnp.dot(masked, remap, precision=lax.Precision.HIGHEST, preferred_element_type=F32)
        if quarter == 2:
            updated_out[...] = anomaly_v[...] + ocean * take(to_tile, 2)

    sent = send_v.at[pl.ds(0, DEVICES - 1)]
    pltpu.make_async_copy(sent, sent, send_sem).wait()
    for moves, _, in_v, gone, _ in (to_block, to_tile):
        for n, (size, _, _, _) in enumerate(moves):
            sent = in_v.at[pl.ds(4 * n, size - 1)]
            pltpu.make_async_copy(sent, sent, gone.at[n]).wait()


def hand_out(a, b, c, d, own, a_out, b_out, c_out, d_out, own_v, sem):
    plane = lax.axis_index("sect") * 4 + lax.div(lax.axis_index("dev"), 16)
    pieces = []
    for k in range(1, 8):
        lanes = pl.ds(pl.multiple_of(lax.rem(plane + k, 8) * 256, 256), 256)
        pieces.append((b.at[:, lanes], b_out.at[:, lanes]))
    pieces += [(a, a_out), (c, c_out), (d, d_out)]
    copies = [pltpu.make_async_copy(source, result, sem.at[i]) for i, (source, result) in enumerate(pieces)]
    for copy in copies:
        copy.start()
    unpack(own, own_v)
    lanes = pl.ds(pl.multiple_of(plane * 256, 256), 256)
    copies.append(pltpu.make_async_copy(own_v, b_out.at[:, lanes], sem.at[len(pieces)]))
    copies[-1].start()
    for copy in copies:
        copy.wait()


def per_device(
    atmosphere_state,
    metric,
    column_group_target,
    physics_input_layer,
    physics_tendency_layer,
    physics_flux_layer,
    block_to_tile,
    remap_weight_matrix,
    ocean_land_mask,
    ocean_sea_anomaly,
    flux_sea_response,
):
    anywhere, vmem, hbm = (pl.BlockSpec(memory_space=space) for space in (pl.ANY, pltpu.VMEM, pltpu.HBM))
    results = [
        jax.ShapeDtypeStruct((WIDTH, COLS), BF16),
        jax.ShapeDtypeStruct((WIDTH, DEVICES * CAP), BF16),
        jax.ShapeDtypeStruct((8, 128), F32),
        jax.ShapeDtypeStruct((8, 128), F32),
    ]
    done = pl.pallas_call(
        kernel,
        out_shape=results + [jax.ShapeDtypeStruct((16, ROWS, 4, 128), BF16)],
        in_specs=[hbm] * 12,
        out_specs=[vmem] * 5,
        scratch_shapes=[
            pltpu.VMEM((8, 128), I32),
            pltpu.VMEM((DEVICES, 384), F32),
            pltpu.VMEM((WIDTH, HID), BF16),
            pltpu.VMEM((WIDTH, COLS), BF16),
            pltpu.VMEM((2, COLS), F32),
            pltpu.VMEM((WIDTH + 16, HID), BF16),
            pltpu.VMEM((4, HID), BF16),
            pltpu.VMEM((1, 4), F32),
            pltpu.VMEM((8, 128), I32),
            pltpu.VMEM((8, 128), I32),
            pltpu.VMEM((8, 128), F32),
            pltpu.VMEM((128, 128), F32),
            pltpu.VMEM((HID, WIDTH), BF16),
            pltpu.VMEM((WIDTH, COLS), BF16),
            pltpu.VMEM((HID, COLS), BF16),
            pltpu.VMEM((384, COLS), BF16),
            pltpu.VMEM((8, 128), F32),
            pltpu.VMEM((DEVICES, ROWS, 4, 128), BF16),
            pltpu.VMEM((DEVICES, ROWS, 4, 128), BF16),
            pltpu.VMEM((3, 16, 128), BF16),
            pltpu.VMEM((16, 16, 128), BF16),
            pltpu.VMEM((3, 8, 128), F32),
            pltpu.VMEM((16, 8, 128), F32),
            pltpu.SemaphoreType.DMA((15,)),
            pltpu.SemaphoreType.DMA,
            pltpu.SemaphoreType.DMA((8,)),
            pltpu.SemaphoreType.DMA((3,)),
            pltpu.SemaphoreType.DMA((3,)),
            pltpu.SemaphoreType.DMA((3,)),
            pltpu.SemaphoreType.DMA((3,)),
        ],
        compiler_params=pltpu.CompilerParams(
            collective_id=0, has_side_effects=True, vmem_limit_bytes=VMEM_LIMIT
        ),
        name="coupling_interval",
    )(*[pltpu.with_memory_space_constraint(v, pltpu.HBM) for v in (
        column_group_target.reshape(DEVICES, 8, 128),
        jnp.asarray(tables()),
        physics_input_layer,
        atmosphere_state.reshape(WIDTH, COLS),
        metric,
        physics_tendency_layer.T,
        physics_flux_layer.T,
        flux_sea_response.reshape(1, 4),
        block_to_tile.reshape(8, 128),
        ocean_land_mask,
        ocean_sea_anomaly,
        remap_weight_matrix,
    )])
    stepped, layout, updated, atmos = pl.pallas_call(
        hand_out,
        out_shape=results,
        in_specs=[anywhere] * 4 + [vmem],
        out_specs=[anywhere] * 4,
        scratch_shapes=[pltpu.VMEM((WIDTH, 256), BF16), pltpu.SemaphoreType.DMA((11,))],
        compiler_params=pltpu.CompilerParams(vmem_limit_bytes=4 * 1024 * 1024),
        name="hand_out",
    )(*done)
    return (
        stepped.reshape(atmosphere_state.shape),
        layout.T,
        updated,
        atmos.reshape(COLS),
    )


def solution(mesh):
    placed = (
        P(None, None, ("sect", "dev")),
        P(None, ("sect", "dev")),
        P(),
        P(),
        P(),
        P(),
        P(),
        P(),
        P(("sect", "dev"), None),
        P(("sect", "dev"), None),
        P(),
    )
    return jax.shard_map(
        per_device,
        mesh=mesh,
        in_specs=placed,
        out_specs=(
            P(None, None, ("sect", "dev")),
            P(("sect", "dev"), None),
            P(("sect", "dev"), None),
            P(("sect", "dev")),
        ),
        check_vma=False,
    )
```

```python
import functools
import itertools
import random

import jax
import jax.numpy as jnp
import numpy as np
from jax import lax
from jax.experimental import pallas as pl
from jax.experimental.pallas import tpu as pltpu
from jax.sharding import PartitionSpec as P

MESH = pl.DeviceIdType.MESH
BF16 = jnp.bfloat16
F32 = jnp.float32
I32 = jnp.int32

DEVICES = 128
CAP = 16
COLS = 1024
WIDTH = 288
HID = 1024
ROWS = 9
STEP = 256
WIDE = 512
EARLY = 5
VMEM_LIMIT = 32 * 1024 * 1024
NT = (((1,), (1,)), ((), ()))


def gll_tables():
    gll_nodes = np.array([-1.0, -1.0 / np.sqrt(5.0), 1.0 / np.sqrt(5.0), 1.0])
    offdiag = gll_nodes[:, None] - gll_nodes[None, :] + np.eye(4)
    bary = np.prod(offdiag, axis=1)
    derivative = bary[:, None] / (bary[None, :] * offdiag)
    diag_sum = np.sum(1.0 / offdiag - np.eye(4), axis=1)
    derivative = derivative * (1.0 - np.eye(4)) + np.eye(4) * diag_sum[:, None]
    first_dir = np.kron(np.eye(8), np.kron(np.eye(4), derivative)).T
    second_dir = np.kron(np.eye(8), np.kron(derivative, np.eye(4))).T
    return np.concatenate([first_dir, second_dir], axis=1)


QUARTERS = [[(0, 1), (0, 3)], [(1, 1), (1, 3)], [(0, 2), (1, 2), (1, 0)], [(0, 0)]]
ARRIVALS = [[(0, 1), (0, 3)], [(1, 1), (1, 3)], [(0, 2), (1, 2)], [(1, 0), (0, 0)]]


def message_order():
    hops = lambda k: min(k, 4 - k)
    mixed, order = random.Random(1), []
    for planes in QUARTERS:
        part = [plane + yz for plane in planes for yz in itertools.product(range(4), range(4))]
        mixed.shuffle(part)
        part.sort(key=lambda o: (o == SELF, -sum(hops(k) for k in o[1:])))
        order += part
    return order


SELF = (0, 0, 0, 0)
ORDER = message_order()
FAR_FIRST = sorted(ORDER, key=lambda o: -sum(min(k, 4 - k) for k in o[1:]))
DIRECT = [16, 16]
CHUNKS = [32, 32, 32]


def tables():
    table = np.zeros((DEVICES, 384), np.float32)
    table[:, :256] = gll_tables()
    table[:, 256:260] = ORDER
    return table


def device(index):
    return (lax.div(index, 64), lax.rem(index, 64))


def dot(a, b):
    return jnp.dot(a, b, preferred_element_type=F32)


def dot_nt(a, b, precision=None):
    return lax.dot_general(a, b, NT, precision=precision, preferred_element_type=F32)


def iota(shape, dim):
    return lax.broadcasted_iota(I32, shape, dim)


def one_hot(condition):
    return jnp.where(condition, 1.0, 0.0).astype(BF16)


def unpack(messages, lanes_out):
    unit = one_hot(iota((256, 256), 0) == iota((256, 256), 1))
    slot, row = iota((256, 64), 0), iota((256, 64), 1)
    spread = one_hot((row >> 2 == slot >> 4) & ((row & 3) == (slot & 3)))
    held = (iota((256, 128), 0) & 15) >> 2 == iota((256, 128), 1) >> 5
    fold = one_hot(iota((32, 128), 0) == (iota((32, 128), 1) & 31))
    main = jnp.concatenate([messages[:, h : h + 4].reshape(256, 128) for h in (0, 4)], axis=1)
    lanes_out[0:256, :] = dot_nt(unit, main).astype(BF16)
    wide = jnp.where(held, dot(spread, messages[:, 8].reshape(64, 128)), 0.0).astype(BF16)
    lanes_out[256:288, :] = dot_nt(fold, wide).astype(BF16)


def kernel(
    target_hbm,
    table_hbm,
    w1_hbm,
    state_hbm,
    metric_hbm,
    w2t_hbm,
    w3t_hbm,
    response_hbm,
    tile_hbm,
    mask_hbm,
    anomaly_hbm,
    remap_hbm,
    stepped_out,
    layout_out,
    updated_out,
    atmos_out,
    own_out,
    target_v,
    table_v,
    w1_v,
    x_v,
    metric_v,
    w23_v,
    w3t_v,
    response_v,
    tile_v,
    mask_v,
    anomaly_v,
    remap_v,
    w1t_v,
    adv_v,
    hid_v,
    tend_v,
    q_v,
    send_v,
    recv_v,
    ocean_out,
    ocean_in,
    cell_out,
    cell_in,
    in_sem,
    send_sem,
    recv_sem,
    ocean_sent,
    ocean_came,
    cell_sent,
    cell_came,
):
    core, chip = lax.axis_index("sect"), lax.axis_index("dev")
    me = core * 64 + chip
    x, y, z = lax.div(chip, 16), lax.rem(lax.div(chip, 4), 4), lax.rem(chip, 4)

    half = COLS // 2
    pairs = [
        (target_hbm.at[me], target_v),
        (table_hbm, table_v),
        (metric_hbm, metric_v),
        (state_hbm.at[:, pl.ds(0, half)], x_v.at[:, pl.ds(0, half)]),
        (state_hbm.at[:, pl.ds(half, half)], x_v.at[:, pl.ds(half, half)]),
        (w1_hbm.at[:, pl.ds(0, half)], w1_v.at[:, pl.ds(0, half)]),
        (w1_hbm.at[:, pl.ds(half, half)], w1_v.at[:, pl.ds(half, half)]),
        (w2t_hbm.at[:, pl.ds(0, half)], w23_v.at[pl.ds(0, WIDTH), pl.ds(0, half)]),
        (w2t_hbm.at[:, pl.ds(half, half)], w23_v.at[pl.ds(0, WIDTH), pl.ds(half, half)]),
        (w3t_hbm, w3t_v),
        (response_hbm, response_v),
        (tile_hbm, tile_v),
        (mask_hbm, mask_v),
        (anomaly_hbm, anomaly_v),
        (remap_hbm, remap_v),
    ]
    loads = [pltpu.make_async_copy(a, b, in_sem.at[i]) for i, (a, b) in enumerate(pairs)]
    for load in loads:
        load.start()

    cores = [lax.rem(core + k, 2) for k in range(2)]
    xs = [lax.rem(x + k, 4) * 16 for k in range(4)]
    ys = [lax.rem(y + k, 4) * 4 for k in range(4)]
    zs = [lax.rem(z + k, 4) for k in range(4)]
    barrier = pltpu.get_barrier_semaphore()
    for a, b, e, f in FAR_FIRST:
        if (a, b, e, f) != SELF:
            pl.semaphore_signal(barrier, inc=1, device_id=(cores[a], xs[b] + ys[e] + zs[f]), device_id_type=MESH)

    for load in loads[0:5]:
        load.wait()
    deriv = table_v[:, 0:256].astype(BF16)

    def dynamics(b):
        at = slice(b * 128, (b + 1) * 128)
        field = x_v[:, at]
        grads = dot(field, deriv)
        wide = field.astype(F32)
        wind_first = wide[0:72] * metric_v[0:1, at]
        wind_second = wide[72:144] * metric_v[1:2, at]
        moved = (
            wide
            - jnp.concatenate([wind_first] * 4, axis=0) * grads[:, 0:128]
            - jnp.concatenate([wind_second] * 4, axis=0) * grads[:, 128:256]
        )
        adv_v[:, at] = moved.astype(BF16)

    def first_layer(c, b):
        at, rows = slice(c * WIDE, (c + 1) * WIDE), slice(b * 256, (b + 1) * 256)
        half = 0.5 * dot(w1t_v[rows, :], adv_v[:, at])
        hid_v[rows, at] = (half + half * jnp.tanh(half)).astype(BF16)

    def second_layer(c):
        at = slice(c * WIDE, (c + 1) * WIDE)
        result = dot(w23_v[...], hid_v[:, at])
        tendency = result[0:WIDTH]
        stepped_out[:, at] = (adv_v[:, at].astype(F32) + tendency).astype(BF16)
        tendency = tendency.astype(BF16)
        tend_v[0:WIDTH, at] = tendency
        for g in range(1, 4):
            tend_v[256 + 32 * g : 288 + 32 * g, at] = tendency[256:288]
        flux = result[WIDTH : WIDTH + 8].astype(BF16).astype(F32)
        mixed = sum(response_v[:, k : k + 1] * flux[k : k + 1] for k in range(4))
        for b in range(WIDE // 128):
            j = c * (WIDE // 128) + b
            q_v[j : j + 1, :] = mixed[:, b * 128 : (b + 1) * 128]

    for b in range(COLS // 128):
        dynamics(b)

    order = table_v[:, 256:384].astype(I32)
    to_device = (
        ((order[:, 0:1] + core) & 1) * 64
        + ((order[:, 1:2] + x) & 3) * 16
        + ((order[:, 2:3] + y) & 3) * 4
        + ((order[:, 3:4] + z) & 3)
    )

    targets = jnp.concatenate([target_v[k : k + 1, :] for k in range(8)], axis=1)
    before = one_hot(iota((STEP, STEP), 0) < iota((STEP, STEP), 1))
    message = iota((DEVICES, STEP), 0)
    taken = jnp.zeros((DEVICES, 1), F32)
    slots = []
    for c in range(COLS // STEP):
        hit = to_device == targets[:, c * STEP : (c + 1) * STEP]
        hits = jnp.where(hit, 1.0, 0.0)
        earlier = dot(hits.astype(BF16), before) + taken
        taken = taken + jnp.sum(hits, axis=1, keepdims=True)
        slot = jnp.where(hit, earlier.astype(I32) + CAP * message, 0)
        slots.append(jnp.sum(slot, axis=0, keepdims=True))
    slots = jnp.concatenate(slots, axis=1)

    plane = lax.div(me, 16)

    def lay_out(first, count, main, tail):
        size, into = count * CAP, pl.ds(first, count)
        main = main.astype(BF16)
        send_v[into, 0:4] = main[:, 0:128].reshape(count, 4, 4, 128)
        send_v[into, 4:8] = main[:, 128:256].reshape(count, 4, 4, 128)
        keep = (iota((size, 128), 0) & 15) >> 2 == iota((size, 128), 1) >> 5
        tail = jnp.where(keep, tail, 0.0).reshape(count, CAP, 128)
        tail = tail[:, 0:8] + tail[:, 8:16]
        send_v[into, 8] = (tail[:, 0:4] + tail[:, 4:8]).astype(BF16)

    def issue(first, count):
        for i in range(first, first + count):
            a, b, e, f = ORDER[i]
            if ORDER[i] == SELF:
                pltpu.make_async_copy(send_v.at[i], recv_v.at[me], recv_sem.at[plane]).start()
                continue
            pltpu.make_async_remote_copy(
                send_v.at[i],
                recv_v.at[me],
                send_sem,
                recv_sem.at[plane],
                device_id=(cores[a], xs[b] + ys[e] + zs[f]),
                device_id_type=MESH,
            ).start()

    def pick(first, count):
        return one_hot(iota((count * CAP, COLS), 0) + first * CAP == slots)

    for load in loads[5:]:
        load.wait()
    lane, sub = iota((8, 128), 1), iota((8, 128), 0)
    shift_row = jnp.where(iota((1, 128), 1) < 8, tile_v[0:1, :] >> 3, -1)
    shift_col = jnp.sum(jnp.where(lane == sub, shift_row, 0), axis=1, keepdims=True)

    def steps(devices):
        return [
            (4, z, devices & 3, lambda k: plane * 16 + y * 4 + k),
            (4, y, (devices >> 2) & 3, lambda k: plane * 16 + k * 4 + z),
            (8, plane, devices >> 4, lambda k: k * 16 + y * 4 + z),
        ]

    def pass_on(way, n, rows):
        (moves, out_v, in_v, sent, came) = way
        size, mine, _, peer = moves[n]
        out_v[n] = rows
        in_v[4 * n + mine] = rows
        for k in range(1, size):
            pltpu.make_async_remote_copy(
                out_v.at[n],
                in_v.at[4 * n + mine],
                sent.at[n],
                came.at[n],
                device_id=device(peer(lax.rem(mine + k, size))),
                device_id_type=MESH,
            ).start()

    def take(way, n):
        (moves, _, in_v, _, came) = way
        size, _, source, _ = moves[n]
        got = in_v.at[pl.ds(4 * n, size - 1)]
        pltpu.make_async_copy(got, got, came.at[n]).wait()
        chosen = jnp.zeros(in_v.shape[1:], F32)
        for k in range(size):
            chosen = chosen + jnp.where(source == k, in_v[4 * n + k].astype(F32), 0.0)
        return chosen

    tile_device = (me + jnp.concatenate([shift_col, shift_col], axis=0)) & (DEVICES - 1)
    block_device = (me - shift_col) & (DEVICES - 1)
    to_block = (steps(tile_device), ocean_out, ocean_in, ocean_sent, ocean_came)
    to_tile = (steps(block_device), cell_out, cell_in, cell_sent, cell_came)
    ocean = mask_v[...].astype(F32)
    ahead = jnp.concatenate([ocean, ocean * anomaly_v[...]], axis=0).astype(BF16)

    w2_tail = jnp.concatenate([w23_v[256:288, :]] * 4, axis=0)
    late = x + y + z >= EARLY
    first = 0
    for count in DIRECT:
        field = dot_nt(pick(first, count), adv_v[...]).astype(BF16)
        half = 0.5 * dot(field, w1_v[...])
        hidden = (half + half * jnp.tanh(half)).astype(BF16)
        main, tail = dot_nt(hidden, w23_v[0:256, :]), dot_nt(hidden, w2_tail)
        lay_out(first, count, main, tail)

        @pl.when(late)
        def _():
            if first == 0:
                pl.semaphore_wait(barrier, DEVICES - 1)
                pass_on(to_block, 0, ahead)
            issue(first, count)

        first += count

    unit = one_hot(iota((256, 256), 0) == iota((256, 256), 1))
    for b in range(HID // 256):
        rows = slice(b * 256, (b + 1) * 256)
        w1t_v[rows, :] = dot_nt(unit, w1_v[:, rows]).astype(BF16)

    w3t = w3t_v[...].astype(F32)
    w23_v[WIDTH : WIDTH + 16, :] = jnp.concatenate([w3t, jnp.zeros((12, HID), F32)], axis=0).astype(BF16)
    for c in range(COLS // WIDE):
        for b in range(HID // 256):
            first_layer(c, b)
        if c > 0:
            second_layer(c - 1)
    second_layer(COLS // WIDE - 1)

    remap = remap_v[...]
    cell = dot_nt(q_v[...], remap, lax.Precision.HIGHEST)

    @pl.when(jnp.logical_not(late))
    def _():
        pl.semaphore_wait(barrier, DEVICES - 1)
        pass_on(to_block, 0, ahead)
        issue(0, sum(DIRECT))

    pass_on(to_tile, 0, cell)

    for n, count in enumerate(CHUNKS):
        placed = dot_nt(pick(first, count), tend_v[...])
        lay_out(first, count, placed[:, 0:256], placed[:, 256:384])
        issue(first, count)
        first += count
        if n < 2:
            pass_on(to_block, n + 1, take(to_block, n).astype(BF16))
        if n > 0:
            pass_on(to_tile, n, take(to_tile, n - 1))

    for quarter, planes in enumerate(ARRIVALS):
        groups = [cores[a] * 4 + lax.rem(x - b + 4, 4) for a, b in planes]
        for group in groups:
            got = recv_v.at[pl.ds(pl.multiple_of(group * 16, 16), 16)]
            pltpu.make_async_copy(got, got, recv_sem.at[group]).wait()
        for k, group in enumerate(groups):
            sixteen = pl.ds(pl.multiple_of(group * 16, 16), 16)
            if quarter == len(ARRIVALS) - 1:
                own_out[16 * k : 16 * k + 16] = recv_v[sixteen]
                continue
            lanes = pl.ds(pl.multiple_of(group * 256, 256), 256)
            unpack(recv_v.at[sixteen], layout_out.at[:, lanes])
        if quarter == 1:
            ahead = take(to_block, 2)
            masked = ahead[8:16] + ahead[0:8] * cell
            atmos_out[...] = jnp.dot(masked, remap, precision=lax.Precision.HIGHEST, preferred_element_type=F32)
        if quarter == 2:
            updated_out[...] = anomaly_v[...] + ocean * take(to_tile, 2)

    sent = send_v.at[pl.ds(0, DEVICES - 1)]
    pltpu.make_async_copy(sent, sent, send_sem).wait()
    for moves, _, in_v, gone, _ in (to_block, to_tile):
        for n, (size, _, _, _) in enumerate(moves):
            sent = in_v.at[pl.ds(4 * n, size - 1)]
            pltpu.make_async_copy(sent, sent, gone.at[n]).wait()


def hand_out(a, b, c, d, own, a_out, b_out, c_out, d_out, own_v, sem):
    plane = lax.axis_index("sect") * 4 + lax.div(lax.axis_index("dev"), 16)
    pieces = []
    for k in (1, 2, 3, 5, 6, 7):
        lanes = pl.ds(pl.multiple_of(lax.rem(plane + k, 8) * 256, 256), 256)
        pieces.append((b.at[:, lanes], b_out.at[:, lanes]))
    pieces += [(a, a_out), (c, c_out), (d, d_out)]
    copies = [pltpu.make_async_copy(source, result, sem.at[i]) for i, (source, result) in enumerate(pieces)]
    for copy in copies:
        copy.start()
    for k in range(2):
        unpack(own.at[pl.ds(16 * k, 16)], own_v.at[k])
        lanes = pl.ds(pl.multiple_of(lax.rem(plane + 4 - 4 * k, 8) * 256, 256), 256)
        copies.append(pltpu.make_async_copy(own_v.at[k], b_out.at[:, lanes], sem.at[len(copies)]))
        copies[-1].start()
    for copy in copies:
        copy.wait()


def per_device(
    atmosphere_state,
    metric,
    column_group_target,
    physics_input_layer,
    physics_tendency_layer,
    physics_flux_layer,
    block_to_tile,
    remap_weight_matrix,
    ocean_land_mask,
    ocean_sea_anomaly,
    flux_sea_response,
):
    anywhere, vmem, hbm = (pl.BlockSpec(memory_space=space) for space in (pl.ANY, pltpu.VMEM, pltpu.HBM))
    results = [
        jax.ShapeDtypeStruct((WIDTH, COLS), BF16),
        jax.ShapeDtypeStruct((WIDTH, DEVICES * CAP), BF16),
        jax.ShapeDtypeStruct((8, 128), F32),
        jax.ShapeDtypeStruct((8, 128), F32),
    ]
    done = pl.pallas_call(
        kernel,
        out_shape=results + [jax.ShapeDtypeStruct((32, ROWS, 4, 128), BF16)],
        in_specs=[hbm] * 12,
        out_specs=[vmem] * 5,
        scratch_shapes=[
            pltpu.VMEM((8, 128), I32),
            pltpu.VMEM((DEVICES, 384), F32),
            pltpu.VMEM((WIDTH, HID), BF16),
            pltpu.VMEM((WIDTH, COLS), BF16),
            pltpu.VMEM((2, COLS), F32),
            pltpu.VMEM((WIDTH + 16, HID), BF16),
            pltpu.VMEM((4, HID), BF16),
            pltpu.VMEM((1, 4), F32),
            pltpu.VMEM((8, 128), I32),
            pltpu.VMEM((8, 128), I32),
            pltpu.VMEM((8, 128), F32),
            pltpu.VMEM((128, 128), F32),
            pltpu.VMEM((HID, WIDTH), BF16),
            pltpu.VMEM((WIDTH, COLS), BF16),
            pltpu.VMEM((HID, COLS), BF16),
            pltpu.VMEM((384, COLS), BF16),
            pltpu.VMEM((8, 128), F32),
            pltpu.VMEM((DEVICES, ROWS, 4, 128), BF16),
            pltpu.VMEM((DEVICES, ROWS, 4, 128), BF16),
            pltpu.VMEM((3, 16, 128), BF16),
            pltpu.VMEM((16, 16, 128), BF16),
            pltpu.VMEM((3, 8, 128), F32),
            pltpu.VMEM((16, 8, 128), F32),
            pltpu.SemaphoreType.DMA((15,)),
            pltpu.SemaphoreType.DMA,
            pltpu.SemaphoreType.DMA((8,)),
            pltpu.SemaphoreType.DMA((3,)),
            pltpu.SemaphoreType.DMA((3,)),
            pltpu.SemaphoreType.DMA((3,)),
            pltpu.SemaphoreType.DMA((3,)),
        ],
        compiler_params=pltpu.CompilerParams(
            collective_id=0, has_side_effects=True, vmem_limit_bytes=VMEM_LIMIT
        ),
        name="coupling_interval",
    )(*[pltpu.with_memory_space_constraint(v, pltpu.HBM) for v in (
        column_group_target.reshape(DEVICES, 8, 128),
        jnp.asarray(tables()),
        physics_input_layer,
        atmosphere_state.reshape(WIDTH, COLS),
        metric,
        physics_tendency_layer.T,
        physics_flux_layer.T,
        flux_sea_response.reshape(1, 4),
        block_to_tile.reshape(8, 128),
        ocean_land_mask,
        ocean_sea_anomaly,
        remap_weight_matrix,
    )])
    stepped, layout, updated, atmos = pl.pallas_call(
        hand_out,
        out_shape=results,
        in_specs=[anywhere] * 4 + [vmem],
        out_specs=[anywhere] * 4,
        scratch_shapes=[pltpu.VMEM((2, WIDTH, 256), BF16), pltpu.SemaphoreType.DMA((11,))],
        compiler_params=pltpu.CompilerParams(vmem_limit_bytes=4 * 1024 * 1024),
        name="hand_out",
    )(*done)
    return (
        stepped.reshape(atmosphere_state.shape),
        layout.T,
        updated,
        atmos.reshape(COLS),
    )


def solution(mesh):
    placed = (
        P(None, None, ("sect", "dev")),
        P(None, ("sect", "dev")),
        P(),
        P(),
        P(),
        P(),
        P(),
        P(),
        P(("sect", "dev"), None),
        P(("sect", "dev"), None),
        P(),
    )
    return jax.shard_map(
        per_device,
        mesh=mesh,
        in_specs=placed,
        out_specs=(
            P(None, None, ("sect", "dev")),
            P(("sect", "dev"), None),
            P(("sect", "dev"), None),
            P(("sect", "dev")),
        ),
        check_vma=False,
    )
```
